32 devices in a mesh: ckpt: 2 (over x), dp: 16 (over z, y, core).
Axes of the slice: x: 2, y: 2, z: 4, core: 2. Of those that a mesh axis runs over, the one named last changes fastest.
Arguments:
- img_feats: bfloat16 [4096, 1664], P(('ckpt', 'dp')), parts along dimension 0, may hold values from -6 to 6
- txt_feats: bfloat16 [4096, 1280], P(('ckpt', 'dp')), parts along dimension 0, may hold values from -6 to 6
- w_img: bfloat16 [3328, 1280], P('ckpt'), parts along dimension 0, may hold values from -1 to 1
- w_txt: bfloat16 [2560, 1280], P('ckpt'), parts along dimension 0, may hold values from -1 to 1
- a_img: bfloat16 [1664, 32], replicated, may hold values from -6 to 6
- b_img: bfloat16 [1280, 128], replicated, may hold values from -6 to 6
- a_txt: bfloat16 [1280, 32], replicated, may hold values from -6 to 6
- b_txt: bfloat16 [1280, 128], replicated, may hold values from -6 to 6
Outputs:
- img_sketch: bfloat16 [4096, 4096], P(('ckpt', 'dp')), parts along dimension 0
- txt_sketch: bfloat16 [4096, 4096], P(('ckpt', 'dp')), parts along dimension 0
The draws below stay inside these ranges and needn't reach their ends.
There are 2 independent parts, one for each index of `ckpt`. The reference program is written for one: setup_inputs(seed, part) draws one part's arguments, and reference() takes and returns one part's arrays. A program takes and returns all parts, laid end to end along the dimension named above; an argument that names none is the same for every part. Nothing has to cross between parts.
All inputs are finite; a program needn't handle non-finite values.
Results may differ from the reference program's by a relative error of at most 0.012.
The reference program's roundings to bfloat16 on the way (of `img_emb`, `txt_emb`, `txt_low` and `weights_bf`) count: a program that leaves them out, or rounds other values in their place, can miss the bound.
Values may be sent and summed in bfloat16 or wider, within the bound.
No kernel may reach another device: no remote copies, remote signals or barrier semaphores. Data moves between devices by JAX's collectives and lax.ppermute only.
A program may use at most 128 MiB of HBM per device.

```python
import math
import jax
import jax.numpy as jnp
from jax import lax

VIS = 1664
TXT = 1280
EMB = 1280
KA = 32
KB = 128
PAIRS = 2048


def shared_base(key):
    weight_key = jax.random.fold_in(key, 1)
    common_key = jax.random.fold_in(key, 2)
    common = jax.random.normal(common_key, (TXT,), jnp.float32)
    base_weight = jnp.clip(jax.random.normal(weight_key, (VIS, EMB), jnp.float32), -6.0, 6.0)
    return (common, base_weight)


def row_ramp(high):
    index = jnp.arange(PAIRS, dtype=jnp.int32).astype(jnp.float32)
    return high * index / PAIRS


def draw_img_feats(key, part):
    common, base_weight = shared_base(key)
    own_key = jax.random.fold_in(key, 11)
    values = jax.random.normal(own_key, (PAIRS, VIS), jnp.float32)
    rising = row_ramp(0.2)
    padded = jnp.concatenate([common, jnp.zeros((VIS - TXT,), jnp.float32)])
    values = values + rising[:, None] * padded[None, :]
    return jnp.clip(values, -6.0, 6.0).astype(jnp.bfloat16)


def draw_txt_feats(key, part):
    common, base_weight = shared_base(key)
    own_key = jax.random.fold_in(key, 23)
    values = jax.random.normal(own_key, (PAIRS, TXT), jnp.float32) + 0.2 * common[None, :]
    return jnp.clip(values, -6.0, 6.0).astype(jnp.bfloat16)


def draw_w_img(key, part):
    common, base_weight = shared_base(key)
    values = base_weight * VIS ** (-0.5)
    return jnp.clip(values, -1.0, 1.0).astype(jnp.bfloat16)


def draw_w_txt(key, part):
    common, base_weight = shared_base(key)
    own_key = jax.random.fold_in(key, 41)
    noise = jax.random.normal(own_key, (TXT, EMB), jnp.float32)
    values = (0.8 * base_weight[:TXT] + 0.6 * noise) * TXT ** (-0.5)
    return jnp.clip(values, -1.0, 1.0).astype(jnp.bfloat16)


def scatter_about(stream_key, extent, scale, most, kind=jnp.bfloat16):
    return jnp.clip(scale * jax.random.normal(stream_key, extent, jnp.float32), -most, most).astype(kind)


def setup_inputs(seed: int = 0, part: int = 0) -> dict:
    keys = jax.random.split(jax.random.key(seed), 9)
    part_splits = jax.random.split(jax.random.fold_in(keys[8], part), 9)
    img_feats = draw_img_feats(jax.random.fold_in(jax.random.fold_in(keys[8], part), 71), part)
    txt_feats = draw_txt_feats(jax.random.fold_in(jax.random.fold_in(keys[8], part), 71), part)
    w_img = draw_w_img(jax.random.fold_in(jax.random.fold_in(keys[8], part), 71), part)
    w_txt = draw_w_txt(jax.random.fold_in(jax.random.fold_in(keys[8], part), 71), part)
    a_img = scatter_about(keys[4], (VIS, KA), 1.0, 6.0)
    b_img = scatter_about(keys[5], (EMB, KB), 1.0, 6.0)
    a_txt = scatter_about(keys[6], (TXT, KA), 1.0, 6.0)
    b_txt = scatter_about(keys[7], (EMB, KB), 1.0, 6.0)
    return {"img_feats": img_feats, "txt_feats": txt_feats, "w_img": w_img, "w_txt": w_txt, "a_img": a_img, "b_img": b_img, "a_txt": a_txt, "b_txt": b_txt}


LOGIT_SCALE = 100.0
EPSILON = 1e-06

def embed(feats, weight):
    raw = jnp.dot(feats, weight, preferred_element_type=jnp.float32)
    inverse = lax.rsqrt(lax.optimization_barrier(jnp.sum(raw * raw, axis=1)) + EPSILON)
    return ((raw * inverse[:, None]).astype(jnp.bfloat16), inverse)

def lse_rows(scores):
    top = lax.optimization_barrier(jnp.max(scores, axis=1))
    return top + jnp.log(lax.optimization_barrier(jnp.sum(jnp.exp(scores - top[:, None]), axis=1)))

def reference(img_feats, txt_feats, w_img, w_txt, a_img, b_img, a_txt, b_txt):
    img_emb, img_inv = embed(img_feats, w_img)
    txt_emb, txt_inv = embed(txt_feats, w_txt)
    img_low = jnp.dot(img_emb, b_img, preferred_element_type=jnp.float32)
    txt_low = jnp.dot(txt_emb, b_img, preferred_element_type=jnp.float32).astype(jnp.bfloat16)
    img_side = jnp.dot(img_emb, b_txt, preferred_element_type=jnp.float32).astype(jnp.bfloat16)
    txt_side = jnp.dot(txt_emb, b_txt, preferred_element_type=jnp.float32)
    img_keys = jnp.dot(img_feats, a_img, preferred_element_type=jnp.float32)
    txt_keys = jnp.dot(txt_feats, a_txt, preferred_element_type=jnp.float32)
    diagonal = lax.optimization_barrier(jnp.sum(img_emb.astype(jnp.float32) * txt_emb.astype(jnp.float32), axis=1))
    block = math.gcd(PAIRS, 1024)
    count = PAIRS // block

    def row_pass(rows):
        return lse_rows(LOGIT_SCALE * jnp.dot(rows, txt_emb.T, preferred_element_type=jnp.float32))

    def col_pass(cols):
        return lse_rows(LOGIT_SCALE * jnp.dot(cols, img_emb.T, preferred_element_type=jnp.float32))
    row_lse = lax.map(row_pass, img_emb.reshape(count, block, EMB)).reshape(PAIRS)
    col_lse = lax.map(col_pass, txt_emb.reshape(count, block, EMB)).reshape(PAIRS)

    def step(carry, pieces):
        partial_value, colsum = carry
        rows, lse_here, low_here, inv_here, diag_here, keys_here, side_here, own_low = pieces
        raw = jnp.dot(rows, txt_emb.T, preferred_element_type=jnp.float32)
        scores = LOGIT_SCALE * raw
        weights = jnp.exp(scores - lse_here[:, None]) + jnp.exp(scores - col_lse[None, :])
        weights_bf = weights.astype(jnp.bfloat16)
        carried = jnp.dot(weights_bf, txt_low, preferred_element_type=jnp.float32)
        inner = lax.optimization_barrier(jnp.sum(weights * raw, axis=1)) - 2.0 * diag_here
        grad = (carried - 2.0 * own_low.astype(jnp.float32) - inner[:, None] * low_here) * inv_here[:, None]
        sketch = (keys_here[:, :, None] * grad[:, None, :]).reshape(block, KA * KB).astype(jnp.bfloat16)
        partial_value = partial_value + jnp.dot(weights_bf.T, side_here, preferred_element_type=jnp.float32)
        colsum = colsum + lax.optimization_barrier(jnp.sum(weights * raw, axis=0))
        return ((partial_value, colsum), sketch)
    init = (jnp.zeros((PAIRS, KB), jnp.float32), jnp.zeros((PAIRS,), jnp.float32))
    pieces = (img_emb.reshape(count, block, EMB), row_lse.reshape(count, block), img_low.reshape(count, block, KB), img_inv.reshape(count, block), diagonal.reshape(count, block), img_keys.reshape(count, block, KA), img_side.reshape(count, block, KB), txt_low.reshape(count, block, KB))
    (partial_value, colsum), sketches = lax.scan(step, init, pieces)
    img_sketch = sketches.reshape(PAIRS, KA * KB)
    inner_txt = colsum - 2.0 * diagonal
    txt_grad = (partial_value - 2.0 * img_side.astype(jnp.float32) - inner_txt[:, None] * txt_side) * txt_inv[:, None]
    txt_sketch = (txt_keys[:, :, None] * txt_grad[:, None, :]).reshape(PAIRS, KA * KB).astype(jnp.bfloat16)
    return (img_sketch, txt_sketch)
```

```python
import jax
import jax.numpy as jnp
from jax import lax
from jax.sharding import PartitionSpec as P

LOGIT_SCALE = 100.0
EPSILON = 1e-06


def embed(feats, weight):
    raw = jnp.dot(feats, weight, preferred_element_type=jnp.float32)
    inverse = lax.rsqrt(jnp.sum(raw * raw, axis=1) + EPSILON)
    return ((raw * inverse[:, None]).astype(jnp.bfloat16), inverse)


def against(left, right):
    return lax.dot_general(
        left, right, (((1,), (1,)), ((), ())), preferred_element_type=jnp.float32
    )


def split_bits(n):
    bits = [1 << b for b in range(n.bit_length() - 1)]
    assert 1 << len(bits) == n
    half = len(bits) // 2
    return bits[: half : -1] + bits[:1], bits[half : 0 : -1]


def swap(x, bit, n):
    return lax.ppermute(x, "dp", [(i, i ^ bit) for i in range(n)])


def gather(block, bits, n):
    blocks = [block]
    for bit in bits:
        blocks = blocks + [swap(b, bit, n) for b in blocks]
    return jnp.concatenate(blocks, axis=0)


def merge_lse(lse, bits, n):
    for j, bit in enumerate(bits):
        other = swap(lse, bit, n)
        cut = other.reshape(-1, 2, 1 << j, lse.shape[1])
        lse = jnp.logaddexp(lse, cut[:, ::-1].reshape(lse.shape))
    return lse


def halve(part, bits, n):
    for bit in reversed(bits):
        half = part.shape[0] // 2
        part = part[:half] + swap(part[half:], bit, n)
    return part


def lse_of(scores, axis):
    top = jnp.max(scores, axis=axis)
    return top + jnp.log(jnp.sum(jnp.exp(scores - jnp.expand_dims(top, axis)), axis=axis))


def body(n, img_feats, txt_feats, w_img, w_txt, a_img, b_img, a_txt, b_txt):
    rows_here = img_feats.shape[0]
    img_bits, txt_bits = split_bits(n)
    txt_emb, txt_inv = embed(txt_feats, w_txt)
    img_emb, img_inv = embed(img_feats, w_img)
    texts = gather(txt_emb, txt_bits, n)
    images = gather(img_emb, img_bits, n)
    diagonal = jnp.sum(img_emb.astype(jnp.float32) * txt_emb.astype(jnp.float32), axis=1)
    img_keys = jnp.dot(img_feats, a_img, preferred_element_type=jnp.float32)
    txt_keys = jnp.dot(txt_feats, a_txt, preferred_element_type=jnp.float32)
    img_low = jnp.dot(images, b_img, preferred_element_type=jnp.float32)
    txt_low = jnp.dot(texts, b_img, preferred_element_type=jnp.float32).astype(jnp.bfloat16)
    img_side = jnp.dot(images, b_txt, preferred_element_type=jnp.float32).astype(jnp.bfloat16)
    txt_side = jnp.dot(texts, b_txt, preferred_element_type=jnp.float32)
    raw = against(images, texts)
    scores = LOGIT_SCALE * raw
    row_lse = merge_lse(lse_of(scores, 1).reshape(-1, rows_here), img_bits, n).reshape(-1)
    col_lse = merge_lse(lse_of(scores, 0).reshape(-1, rows_here), txt_bits, n).reshape(-1)
    weights = jnp.exp(scores - row_lse[:, None]) + jnp.exp(scores - col_lse[None, :])
    weights_bf = weights.astype(jnp.bfloat16)
    weighted = weights * raw
    img_part = (
        jnp.dot(weights_bf, txt_low, preferred_element_type=jnp.float32)
        - jnp.sum(weighted, axis=1)[:, None] * img_low
    )
    txt_part = (
        lax.dot_general(
            weights_bf, img_side, (((0,), (0,)), ((), ())), preferred_element_type=jnp.float32
        )
        - jnp.sum(weighted, axis=0)[:, None] * txt_side
    )
    img_sum = halve(img_part, img_bits, n)
    txt_sum = halve(txt_part, txt_bits, n)
    twice = 2.0 * diagonal[:, None]
    own = slice(0, rows_here)
    img_grad = (img_sum - 2.0 * txt_low[own].astype(jnp.float32) + twice * img_low[own]) * img_inv[:, None]
    txt_grad = (txt_sum - 2.0 * img_side[own].astype(jnp.float32) + twice * txt_side[own]) * txt_inv[:, None]
    return tuple(
        (keys[:, :, None] * grad[:, None, :]).reshape(rows_here, -1).astype(jnp.bfloat16)
        for keys, grad in ((img_keys, img_grad), (txt_keys, txt_grad))
    )


def solution(mesh):
    n = mesh.shape["dp"]
    rows = P(("ckpt", "dp"), None)
    part = P("ckpt", None)
    return jax.shard_map(
        lambda *args: body(n, *args),
        mesh=mesh,
        in_specs=(rows, rows, part, part, P(), P(), P(), P()),
        out_specs=(rows, rows),
        check_vma=False,
    )
```

```python
import functools
import jax
import jax.numpy as jnp
from jax import lax
from jax.experimental import pallas as pl
from jax.experimental.pallas import tpu as pltpu
from jax.sharding import PartitionSpec as P

LOGIT_SCALE = 100.0
EPSILON = 1e-06
F32 = jnp.float32
BF16 = jnp.bfloat16
LANES = 128


def dot(left, right, left_dim=1, right_dim=0):
    return lax.dot_general(
        left, right, (((left_dim,), (right_dim,)), ((), ())), preferred_element_type=F32
    )


def call(kernel, outs, args, scratch=(), flops=0, limit=32):
    args = [pltpu.with_memory_space_constraint(a, pltpu.VMEM) for a in args]
    size = sum(a.size * a.dtype.itemsize for a in args)
    return pl.pallas_call(
        kernel,
        out_shape=[jax.ShapeDtypeStruct(s, d) for s, d in outs],
        in_specs=[pl.BlockSpec(memory_space=pltpu.VMEM)] * len(args),
        out_specs=[pl.BlockSpec(memory_space=pltpu.VMEM)] * len(outs),
        scratch_shapes=list(scratch),
        compiler_params=pltpu.CompilerParams(vmem_limit_bytes=limit << 20),
        cost_estimate=pl.CostEstimate(flops=flops, bytes_accessed=size, transcendentals=0),
    )(*args)


def span(bits):
    offsets = [0]
    for bit in bits:
        offsets = offsets + [o ^ bit for o in offsets]
    return offsets


def split_bits(n):
    bits = [1 << b for b in range(n.bit_length() - 1)]
    assert 1 << len(bits) == n
    half = len(bits) // 2
    return bits[:half:-1] + bits[:1], bits[half:0:-1]


def swap(x, offset, n):
    return lax.ppermute(x, "dp", [(i, i ^ offset) for i in range(n)])


def gather(block, bits, n):
    blocks = [block]
    for bit in bits:
        blocks = blocks + [swap(b, bit, n) for b in blocks]
    return blocks


def embed_kernel(feats, weight, *rest):
    raw = dot(feats[...], weight[...])
    inverse = lax.rsqrt(jnp.sum(raw * raw, axis=1, keepdims=True) + EPSILON)
    if len(rest) == 3:
        factor, emb, keys = rest
        keys[...] = dot(feats[...], factor[...]) * inverse
    else:
        (emb,) = rest
    emb[...] = (raw * inverse).astype(BF16)


def embed(feats, weight, factor=None):
    rows, emb = feats.shape[0], weight.shape[1]
    outs = [((rows, emb), BF16)]
    args = [feats, weight]
    if factor is not None:
        outs.append(((rows, factor.shape[1]), F32))
        args.append(factor)
    return call(embed_kernel, outs, args, flops=2 * rows * weight.size)


def column_of(row):
    return jnp.broadcast_to(row, (LANES, LANES)).T


def scores_kernel(ni, nt, *refs):
    images, texts = refs[:ni], refs[ni : ni + nt]
    raw, row_lse, col_lse, all_images, all_texts = refs[ni + nt :]
    rows = images[0].shape[0]
    for a in range(ni):
        all_images[a * rows : (a + 1) * rows] = images[a][...]
    for t in range(nt):
        all_texts[t * rows : (t + 1) * rows] = texts[t][...]
    raw[...] = dot(all_images[...], all_texts[...], 1, 1)
    for a in range(ni):
        scores = LOGIT_SCALE * raw[a * rows : (a + 1) * rows]
        top = jnp.max(scores, axis=1, keepdims=True)
        lse = top + jnp.log(jnp.sum(jnp.exp(scores - top), axis=1, keepdims=True))
        row_lse[a : a + 1] = jnp.broadcast_to(lse, (rows, LANES)).T[:1]
    for t in range(nt):
        scores = LOGIT_SCALE * raw[:, t * rows : (t + 1) * rows]
        top = jnp.max(scores, axis=0, keepdims=True)
        col_lse[t : t + 1] = top + jnp.log(jnp.sum(jnp.exp(scores - top), axis=0, keepdims=True))


def factors_kernel(ni, nt, *refs):
    images, texts, (b_img, b_txt) = refs[:ni], refs[ni : ni + nt], refs[ni + nt : ni + nt + 2]
    img_low, img_side_t, txt_low, txt_side_t, img_base, txt_base = refs[ni + nt + 2 :]
    rows = images[0].shape[0]
    for a in range(ni):
        here = slice(a * rows, (a + 1) * rows)
        low = dot(images[a][...], b_img[...])
        side = dot(images[a][...], b_txt[...])
        img_low[here] = low
        img_side_t[:, here] = side.T.astype(BF16)
        if a == 0:
            own_img_low, own_img_side = low, side.astype(BF16).astype(F32)
    for t in range(nt):
        here = slice(t * rows, (t + 1) * rows)
        low = dot(texts[t][...], b_img[...]).astype(BF16)
        side = dot(texts[t][...], b_txt[...])
        txt_low[here] = low
        txt_side_t[:, here] = side.T
        if t == 0:
            own_txt_low, own_txt_side = low.astype(F32), side
    diagonal = jnp.sum(
        images[0][...].astype(F32) * texts[0][...].astype(F32), axis=1, keepdims=True
    )
    img_base[...] = 2.0 * (diagonal * own_img_low - own_txt_low)
    txt_base[...] = 2.0 * (diagonal * own_txt_side - own_img_side)


def merge(parts):
    slots = parts[0].shape[0]
    lined = [parts[0][...]]
    for k in range(1, len(parts)):
        lined.append(
            jnp.concatenate([parts[k][s ^ k : (s ^ k) + 1] for s in range(slots)], axis=0)
        )
    top = functools.reduce(jnp.maximum, lined)
    return top + jnp.log(sum(jnp.exp(p - top) for p in lined))


def weights_kernel(ni, nt, *refs):
    row_parts, col_parts = refs[:ni], refs[ni : ni + nt]
    raw, img_low, img_side_t, txt_low, txt_side_t = refs[ni + nt : ni + nt + 5]
    img_parts = refs[ni + nt + 5 : 2 * ni + nt + 5]
    txt_parts = refs[2 * ni + nt + 5 : 2 * ni + 2 * nt + 5]
    weights_bf = refs[-1]
    rows = LANES
    row_lse = merge(row_parts)
    col_lse = merge(col_parts)
    inner_col = [jnp.zeros((1, rows), F32) for _ in range(nt)]
    for a in range(ni):
        row = column_of(row_lse[a : a + 1])
        inner_row = jnp.zeros((rows, rows), F32)
        for t in range(nt):
            here = raw[a * rows : (a + 1) * rows, t * rows : (t + 1) * rows]
            scores = LOGIT_SCALE * here
            weights = jnp.exp(scores - row) + jnp.exp(scores - col_lse[t : t + 1])
            weights_bf[a * rows : (a + 1) * rows, t * rows : (t + 1) * rows] = weights.astype(BF16)
            weighted = weights * here
            inner_row = inner_row + weighted
            inner_col[t] = inner_col[t] + jnp.sum(weighted, axis=0, keepdims=True)
        inner = jnp.sum(inner_row, axis=1, keepdims=True)
        img_parts[a][...] = (
            dot(weights_bf[a * rows : (a + 1) * rows], txt_low[...])
            - inner * img_low[a * rows : (a + 1) * rows]
        )
    for t in range(nt):
        here = slice(t * rows, (t + 1) * rows)
        txt_parts[t][...] = dot(img_side_t[...], weights_bf[:, here]) - inner_col[t] * txt_side_t[:, here]


def sketch_kernel(ni, nt, *refs):
    img_parts, txt_parts = refs[:ni], refs[ni : ni + nt]
    img_base, txt_base, img_keys, txt_keys, img_out, txt_out = refs[ni + nt :]
    img_grad = sum((p[...] for p in img_parts), img_base[...])
    txt_grad = sum((p[...] for p in txt_parts[1:]), txt_parts[0][...]).T + txt_base[...]
    for keys, grad, out in ((img_keys, img_grad, img_out), (txt_keys, txt_grad, txt_out)):
        width = grad.shape[1]
        for a in range(keys.shape[1]):
            out[:, a * width : (a + 1) * width] = (keys[:, a : a + 1] * grad).astype(BF16)


def body(n, img_feats, txt_feats, w_img, w_txt, a_img, b_img, a_txt, b_txt):
    rows, wide = img_feats.shape[0], w_img.shape[1]
    low = b_img.shape[1]
    assert rows == LANES and low == LANES
    img_bits, txt_bits = split_bits(n)
    img_span, txt_span = span(img_bits), span(txt_bits)
    ni, nt = len(img_span), len(txt_span)
    feats = gather(txt_feats, txt_bits, n)
    img_emb, img_keys = embed(img_feats, w_img, a_img)
    images = gather(img_emb, img_bits, n)
    txt_emb, txt_keys = embed(txt_feats, w_txt, a_txt)
    texts = [txt_emb] + [embed(f, w_txt)[0] for f in feats[1:]]
    raw, row_lse, col_lse = call(
        functools.partial(scores_kernel, ni, nt),
        [((ni * rows, nt * rows), F32), ((ni, rows), F32), ((nt, rows), F32)],
        images + texts,
        scratch=[pltpu.VMEM((ni * rows, wide), BF16), pltpu.VMEM((nt * rows, wide), BF16)],
        flops=2 * ni * nt * rows * rows * wide,
    )
    row_parts = [row_lse] + [swap(row_lse, o, n) for o in img_span[1:]]
    col_parts = [col_lse] + [swap(col_lse, o, n) for o in txt_span[1:]]
    img_low, img_side_t, txt_low, txt_side_t, img_base, txt_base = call(
        functools.partial(factors_kernel, ni, nt),
        [
            ((ni * rows, low), F32),
            ((low, ni * rows), BF16),
            ((nt * rows, low), BF16),
            ((low, nt * rows), F32),
            ((rows, low), F32),
            ((rows, low), F32),
        ],
        images + texts + [b_img, b_txt],
        flops=4 * (ni + nt) * rows * wide * low,
    )
    parts = call(
        functools.partial(weights_kernel, ni, nt),
        [((rows, low), F32)] * (ni + nt),
        row_parts + col_parts + [raw, img_low, img_side_t, txt_low, txt_side_t],
        scratch=[pltpu.VMEM((ni * rows, nt * rows), BF16)],
        flops=4 * ni * nt * rows * rows * low,
    )
    img_parts, txt_parts = parts[:ni], parts[ni:]
    img_parts = [img_parts[0]] + [swap(p, o, n) for p, o in zip(img_parts[1:], img_span[1:])]
    txt_parts = [txt_parts[0]] + [swap(p, o, n) for p, o in zip(txt_parts[1:], txt_span[1:])]
    return tuple(
        call(
            functools.partial(sketch_kernel, ni, nt),
            [((rows, img_keys.shape[1] * low), BF16), ((rows, txt_keys.shape[1] * low), BF16)],
            img_parts + txt_parts + [img_base, txt_base, img_keys, txt_keys],
        )
    )


def solution(mesh):
    n = mesh.shape["dp"]
    rows = P(("ckpt", "dp"), None)
    part = P("ckpt", None)
    return jax.shard_map(
        lambda *args: body(n, *args),
        mesh=mesh,
        in_specs=(rows, rows, part, part, P(), P(), P(), P()),
        out_specs=(rows, rows),
        check_vma=False,
    )
```

```python
import functools
import jax
import jax.numpy as jnp
from jax import lax
from jax.experimental import pallas as pl
from jax.experimental.pallas import tpu as pltpu
from jax.sharding import PartitionSpec as P

LOGIT_SCALE = 100.0
EPSILON = 1e-06
F32 = jnp.float32
BF16 = jnp.bfloat16
LANES = 128
PIECES = 4


def dot(left, right, left_dim=1, right_dim=0):
    return lax.dot_general(
        left, right, (((left_dim,), (right_dim,)), ((), ())), preferred_element_type=F32
    )


def skip(kernel, first, count, *refs):
    kernel(*refs[:first], *refs[first + count :])


def call(kernel, outs, args, after=(), free=(), scratch=(), flops=0, limit=16):
    args = [a if k in free else pltpu.with_memory_space_constraint(a, pltpu.VMEM) for k, a in enumerate(args)]
    size = sum(a.size * a.dtype.itemsize for a in args)
    specs = [pl.BlockSpec(memory_space=pltpu.VMEM)] * len(args)
    if after:
        kernel = functools.partial(skip, kernel, len(args), len(after))
        args, specs = args + list(after), specs + [pl.BlockSpec(memory_space=pl.ANY)] * len(after)
    return pl.pallas_call(
        kernel,
        out_shape=[jax.ShapeDtypeStruct(s, d) for s, d in outs],
        in_specs=specs,
        out_specs=[pl.BlockSpec(memory_space=pltpu.VMEM)] * len(outs),
        scratch_shapes=list(scratch),
        compiler_params=pltpu.CompilerParams(vmem_limit_bytes=limit << 20),
        cost_estimate=pl.CostEstimate(flops=flops, bytes_accessed=size, transcendentals=0),
    )(*args)


def span(bits):
    offsets = [0]
    for bit in bits:
        offsets = offsets + [o ^ bit for o in offsets]
    return offsets


def split_bits(n):
    bits = [1 << b for b in range(n.bit_length() - 1)]
    assert 1 << len(bits) == n
    half = len(bits) // 2
    return bits[:half:-1] + bits[:1], bits[half:0:-1]


def swap(x, offset, n):
    return lax.ppermute(x, "dp", [(i, i ^ offset) for i in range(n)])


def gather(block, bits, n, ready=lambda x: x):
    blocks, sent = [block], [block]
    for bit in bits:
        new = [swap(b, bit, n) for b in sent]
        blocks, sent = blocks + new, sent + [ready(b) for b in new]
    return blocks


def normalised(raw):
    inverse = lax.rsqrt(jnp.sum(raw * raw, axis=1, keepdims=True) + EPSILON)
    return (raw * inverse).astype(BF16), inverse


def embed_kernel(blocks, *refs):
    feats, weight, embs = refs[:blocks], refs[blocks], refs[blocks + 1 :]
    for b in range(blocks):
        embs[b][...] = normalised(dot(feats[b][...], weight[...]))[0]


def embed(feats, weight):
    rows, blocks = feats[0].shape[0], len(feats)
    return list(
        call(
            functools.partial(embed_kernel, blocks),
            [((rows, weight.shape[1]), BF16)] * blocks,
            [*feats, weight],
            flops=2 * blocks * rows * weight.size,
        )
    )


def stream_kernel(blocks, cuts, *refs):
    feats, weight, embs = refs[:blocks], refs[blocks], refs[blocks + 1 : 2 * blocks + 1]
    inverse, weight_v, own_v, sems = refs[2 * blocks + 1 :]
    own = pltpu.make_async_copy(feats[0], own_v, sems.at[0])
    pieces = [slice(lo, hi) for lo, hi in zip(cuts, cuts[1:])]
    copies = [
        pltpu.make_async_copy(weight.at[p], weight_v.at[p], sems.at[1 + k]) for k, p in enumerate(pieces)
    ]
    for copy in [own, *copies]:
        copy.start()
    own.wait()
    raws = [0.0] * blocks
    for p, copy in zip(pieces, copies):
        copy.wait()
        for b in range(blocks):
            left = own_v[:, p] if b == 0 else feats[b][:, p]
            raws[b] = raws[b] + dot(left, weight_v[p])
    embs[0][...], inverse[...] = normalised(raws[0])
    for b in range(1, blocks):
        embs[b][...] = normalised(raws[b])[0]


def stream_embed(feats, weight, keep):
    (rows, depth), blocks = feats[0].shape, len(feats)
    cuts = [depth // LANES * k // PIECES * LANES for k in range(PIECES)] + [depth]
    far = [pltpu.with_memory_space_constraint(a, pltpu.HBM) for a in (feats[0], weight)]
    near = [pltpu.with_memory_space_constraint(a, pltpu.VMEM) for a in feats[1:]]
    hbm, vmem = pl.BlockSpec(memory_space=pltpu.HBM), pl.BlockSpec(memory_space=pltpu.VMEM)
    outs = [((rows, weight.shape[1]), BF16)] * blocks + [((rows, 1), F32)] + [(weight.shape, BF16)] * keep
    out = pl.pallas_call(
        functools.partial(stream_kernel, blocks, cuts),
        out_shape=[jax.ShapeDtypeStruct(*o) for o in outs],
        in_specs=[hbm] + [vmem] * (blocks - 1) + [hbm],
        out_specs=[vmem] * len(outs),
        scratch_shapes=[pltpu.VMEM(weight.shape, BF16)] * (not keep)
        + [pltpu.VMEM((rows, depth), BF16), pltpu.SemaphoreType.DMA((PIECES + 1,))],
        compiler_params=pltpu.CompilerParams(vmem_limit_bytes=16 << 20),
        cost_estimate=pl.CostEstimate(
            flops=2 * blocks * rows * weight.size, bytes_accessed=2 * weight.size, transcendentals=0
        ),
    )(far[0], *near, far[1])
    return list(out[:blocks]), *out[blocks:]


def keys_kernel(*refs):
    for feats, factor, inverse, wide in zip(refs[:2], refs[2:4], refs[4:6], refs[6:8]):
        keys = dot(feats[...], factor[...], 1, 1) * inverse[...]
        for a in range(keys.shape[1]):
            wide[:, a * LANES : (a + 1) * LANES] = jnp.broadcast_to(keys[:, a : a + 1], (keys.shape[0], LANES))


def hold(x, after):
    args = [pltpu.with_memory_space_constraint(a, pltpu.VMEM) for a in [x, *after]]
    return pl.pallas_call(
        lambda *refs: None,
        out_shape=jax.ShapeDtypeStruct(x.shape, x.dtype),
        in_specs=[pl.BlockSpec(memory_space=pltpu.VMEM)] * len(args),
        out_specs=pl.BlockSpec(memory_space=pltpu.VMEM),
        input_output_aliases={0: 0},
        compiler_params=pltpu.CompilerParams(vmem_limit_bytes=1 << 20),
    )(*args)


def column_of(row):
    return jnp.broadcast_to(row, (LANES, LANES)).T


def scores_kernel(ni, nt, *refs):
    images, texts = refs[:ni], refs[ni : ni + nt]
    raw, row_lse, col_lse, all_images, all_texts = refs[ni + nt :]
    rows = images[0].shape[0]
    for a in range(ni):
        all_images[a * rows : (a + 1) * rows] = images[a][...]
    for t in range(nt):
        all_texts[t * rows : (t + 1) * rows] = texts[t][...]
    raw[...] = dot(all_images[...], all_texts[...], 1, 1)
    for a in range(ni):
        scores = LOGIT_SCALE * raw[a * rows : (a + 1) * rows]
        top = jnp.max(scores, axis=1, keepdims=True)
        lse = top + jnp.log(jnp.sum(jnp.exp(scores - top), axis=1, keepdims=True))
        row_lse[a : a + 1] = jnp.broadcast_to(lse, (rows, LANES)).T[:1]
    for t in range(nt):
        scores = LOGIT_SCALE * raw[:, t * rows : (t + 1) * rows]
        top = jnp.max(scores, axis=0, keepdims=True)
        col_lse[t : t + 1] = top + jnp.log(jnp.sum(jnp.exp(scores - top), axis=0, keepdims=True))


def factors_kernel(ni, nt, *refs):
    images, texts, (b_img, b_txt) = refs[:ni], refs[ni : ni + nt], refs[ni + nt : ni + nt + 2]
    img_low, img_side_t, txt_low, txt_side_t, img_base, txt_base = refs[ni + nt + 2 :]
    rows = images[0].shape[0]
    for a in range(ni):
        here = slice(a * rows, (a + 1) * rows)
        low = dot(images[a][...], b_img[...])
        side = dot(images[a][...], b_txt[...])
        img_low[here] = low
        img_side_t[:, here] = side.T.astype(BF16)
        if a == 0:
            own_img_low, own_img_side = low, side.astype(BF16).astype(F32)
    for t in range(nt):
        here = slice(t * rows, (t + 1) * rows)
        low = dot(texts[t][...], b_img[...]).astype(BF16)
        side = dot(texts[t][...], b_txt[...])
        txt_low[here] = low
        txt_side_t[:, here] = side.T
        if t == 0:
            own_txt_low, own_txt_side = low.astype(F32), side
    diagonal = jnp.sum(
        images[0][...].astype(F32) * texts[0][...].astype(F32), axis=1, keepdims=True
    )
    img_base[...] = 2.0 * (diagonal * own_img_low - own_txt_low)
    txt_base[...] = 2.0 * (diagonal * own_txt_side - own_img_side)


def merge(parts):
    slots = parts[0].shape[0]
    lined = [parts[0][...]]
    for k in range(1, len(parts)):
        lined.append(
            jnp.concatenate([parts[k][s ^ k : (s ^ k) + 1] for s in range(slots)], axis=0)
        )
    top = functools.reduce(jnp.maximum, lined)
    return top + jnp.log(sum(jnp.exp(p - top) for p in lined))


def weights_kernel(ni, nt, *refs):
    row_parts, col_parts = refs[:ni], refs[ni : ni + nt]
    raw, img_low, img_side_t, txt_low, txt_side_t = refs[ni + nt : ni + nt + 5]
    img_parts = refs[ni + nt + 5 : 2 * ni + nt + 5]
    txt_parts = refs[2 * ni + nt + 5 : 2 * ni + 2 * nt + 5]
    weights_bf = refs[-1]
    rows = LANES
    row_lse = merge(row_parts)
    col_lse = merge(col_parts)
    inner_col = [jnp.zeros((1, rows), F32) for _ in range(nt)]
    for a in range(ni):
        row = column_of(row_lse[a : a + 1])
        inner_row = jnp.zeros((rows, rows), F32)
        for t in range(nt):
            here = raw[a * rows : (a + 1) * rows, t * rows : (t + 1) * rows]
            scores = LOGIT_SCALE * here
            weights = jnp.exp(scores - row) + jnp.exp(scores - col_lse[t : t + 1])
            weights_bf[a * rows : (a + 1) * rows, t * rows : (t + 1) * rows] = weights.astype(BF16)
            weighted = weights * here
            inner_row = inner_row + weighted
            inner_col[t] = inner_col[t] + jnp.sum(weighted, axis=0, keepdims=True)
        inner = jnp.sum(inner_row, axis=1, keepdims=True)
        part = (
            dot(weights_bf[a * rows : (a + 1) * rows], txt_low[...])
            - inner * img_low[a * rows : (a + 1) * rows]
        )
        img_parts[a][...] = part.astype(img_parts[a].dtype)
    for t in range(nt):
        here = slice(t * rows, (t + 1) * rows)
        part = dot(img_side_t[...], weights_bf[:, here]) - inner_col[t] * txt_side_t[:, here]
        txt_parts[t][...] = part.astype(txt_parts[t].dtype)


def sketch_kernel(count, turned, *refs):
    parts, (base, keys, out, made, sems) = refs[:count], refs[count:]
    rows = base.shape[0]
    grad = sum((part[...].astype(F32) for part in parts[1:]), parts[0][...])
    grad = (grad.T if turned else grad) + base[...]
    copies, step = [], rows // 2
    for k in range(2):
        here = slice(k * step, (k + 1) * step)
        for a in range(0, made.shape[1], LANES):
            made[here, a : a + LANES] = (keys[here, a : a + LANES] * grad[here]).astype(BF16)
        copies.append(pltpu.make_async_copy(made.at[here], out.at[here], sems.at[k]))
        copies[-1].start()
    for copy in copies:
        copy.wait()


def sketch(parts, base, keys, turned):
    args = [pltpu.with_memory_space_constraint(a, pltpu.VMEM) for a in [*parts, base, keys]]
    return pl.pallas_call(
        functools.partial(sketch_kernel, len(parts), turned),
        out_shape=jax.ShapeDtypeStruct(keys.shape, BF16),
        in_specs=[pl.BlockSpec(memory_space=pltpu.VMEM)] * len(args),
        out_specs=pl.BlockSpec(memory_space=pltpu.HBM),
        scratch_shapes=[pltpu.VMEM(keys.shape, BF16), pltpu.SemaphoreType.DMA((2,))],
        compiler_params=pltpu.CompilerParams(vmem_limit_bytes=16 << 20),
        cost_estimate=pl.CostEstimate(flops=keys.size, bytes_accessed=6 * keys.size, transcendentals=0),
    )(*args)


def body(n, img_feats, txt_feats, w_img, w_txt, a_img, b_img, a_txt, b_txt):
    rows, wide = img_feats.shape[0], w_img.shape[1]
    low = b_img.shape[1]
    assert rows == LANES and low == LANES
    img_bits, txt_bits = split_bits(n)
    img_span, txt_span = span(img_bits), span(txt_bits)
    ni, nt = len(img_span), len(txt_span)
    (img_emb,), img_inv = stream_embed([img_feats], w_img, False)
    feats = gather(txt_feats, txt_bits, n)
    texts, txt_inv, w_txt_v = stream_embed(feats[:-1], w_txt, True)
    img_keys, txt_keys = call(
        keys_kernel,
        [((rows, a_img.shape[1] * LANES), F32), ((rows, a_txt.shape[1] * LANES), F32)],
        [img_feats, txt_feats, a_img.T, a_txt.T, img_inv, txt_inv],
    )
    images = gather(img_emb, img_bits, n, lambda x: hold(x, [texts[0], img_keys]))
    texts = texts + embed(feats[-1:], w_txt_v)
    raw, row_lse, col_lse = call(
        functools.partial(scores_kernel, ni, nt),
        [((ni * rows, nt * rows), F32), ((ni, rows), F32), ((nt, rows), F32)],
        images + texts,
        scratch=[pltpu.VMEM((ni * rows, wide), BF16), pltpu.VMEM((nt * rows, wide), BF16)],
        flops=2 * ni * nt * rows * rows * wide,
    )
    row_parts = gather(row_lse, img_bits, n)
    col_parts = [col_lse] + [swap(col_lse, o, n) for o in txt_span[1:]]
    img_low, img_side_t, txt_low, txt_side_t, img_base, txt_base = call(
        functools.partial(factors_kernel, ni, nt),
        [
            ((ni * rows, low), F32),
            ((low, ni * rows), BF16),
            ((nt * rows, low), BF16),
            ((low, nt * rows), F32),
            ((rows, low), F32),
            ((rows, low), F32),
        ],
        images + texts + [b_img, b_txt],
        flops=4 * (ni + nt) * rows * wide * low,
    )
    parts = call(
        functools.partial(weights_kernel, ni, nt),
        [((rows, low), F32 if k in (0, ni) else BF16) for k in range(ni + nt)],
        row_parts + col_parts + [raw, img_low, img_side_t, txt_low, txt_side_t],
        scratch=[pltpu.VMEM((ni * rows, nt * rows), BF16)],
        flops=4 * ni * nt * rows * rows * low,
    )
    img_parts, txt_parts = [
        [own] + [swap(p, o, n) for p, o in zip(sent, offsets[1:])]
        for (own, *sent), offsets in ((parts[:ni], img_span), (parts[ni:], txt_span))
    ]
    return (
        sketch(img_parts, img_base, img_keys, False),
        sketch(txt_parts, txt_base, txt_keys, True),
    )


def solution(mesh):
    n = mesh.shape["dp"]
    rows = P(("ckpt", "dp"), None)
    part = P("ckpt", None)
    return jax.shard_map(
        lambda *args: body(n, *args),
        mesh=mesh,
        in_specs=(rows, rows, part, part, P(), P(), P(), P()),
        out_specs=(rows, rows),
        check_vma=False,
    )
```

```python
import functools
import jax
import jax.numpy as jnp
from jax import lax
from jax.experimental import pallas as pl
from jax.experimental.pallas import tpu as pltpu
from jax.sharding import PartitionSpec as P

LOGIT_SCALE = 100.0
EPSILON = 1e-06
F32 = jnp.float32
BF16 = jnp.bfloat16
LANES = 128
PIECES = 4


def dot(left, right, left_dim=1, right_dim=0):
    return lax.dot_general(
        left, right, (((left_dim,), (right_dim,)), ((), ())), preferred_element_type=F32
    )


def skip(kernel, first, count, *refs):
    kernel(*refs[:first], *refs[first + count :])


def call(kernel, outs, args, after=(), free=(), scratch=(), flops=0, limit=16):
    args = [a if k in free else pltpu.with_memory_space_constraint(a, pltpu.VMEM) for k, a in enumerate(args)]
    size = sum(a.size * a.dtype.itemsize for a in args)
    specs = [pl.BlockSpec(memory_space=pltpu.VMEM)] * len(args)
    if after:
        kernel = functools.partial(skip, kernel, len(args), len(after))
        args, specs = args + list(after), specs + [pl.BlockSpec(memory_space=pl.ANY)] * len(after)
    return pl.pallas_call(
        kernel,
        out_shape=[jax.ShapeDtypeStruct(s, d) for s, d in outs],
        in_specs=specs,
        out_specs=[pl.BlockSpec(memory_space=pltpu.VMEM)] * len(outs),
        scratch_shapes=list(scratch),
        compiler_params=pltpu.CompilerParams(vmem_limit_bytes=limit << 20),
        cost_estimate=pl.CostEstimate(flops=flops, bytes_accessed=size, transcendentals=0),
    )(*args)


def span(bits):
    offsets = [0]
    for bit in bits:
        offsets = offsets + [o ^ bit for o in offsets]
    return offsets


def split_bits(n):
    bits = [1 << b for b in range(n.bit_length() - 1)]
    assert 1 << len(bits) == n
    half = len(bits) // 2
    return bits[:half:-1] + bits[:1], bits[half:0:-1]


def swap(x, offset, n):
    return lax.ppermute(x, "dp", [(i, i ^ offset) for i in range(n)])


def gather(block, bits, n, ready=lambda x: x):
    blocks, sent = [block], [block]
    for bit in bits:
        new = [swap(b, bit, n) for b in sent]
        blocks, sent = blocks + new, sent + [ready(b) for b in new]
    return blocks


def normalised(raw):
    inverse = lax.rsqrt(jnp.sum(raw * raw, axis=1, keepdims=True) + EPSILON)
    return (raw * inverse).astype(BF16), inverse


def embed_kernel(blocks, *refs):
    feats, weight, embs = refs[:blocks], refs[blocks], refs[blocks + 1 :]
    for b in range(blocks):
        embs[b][...] = normalised(dot(feats[b][...], weight[...]))[0]


def embed(feats, weight):
    rows, blocks = feats[0].shape[0], len(feats)
    return list(
        call(
            functools.partial(embed_kernel, blocks),
            [((rows, weight.shape[1]), BF16)] * blocks,
            [*feats, weight],
            flops=2 * blocks * rows * weight.size,
        )
    )


def stream_kernel(blocks, cuts, *refs):
    feats, weight, embs = refs[:blocks], refs[blocks], refs[blocks + 1 : 2 * blocks + 1]
    inverse, weight_v, own_v, sems = refs[2 * blocks + 1 :]
    own = pltpu.make_async_copy(feats[0], own_v, sems.at[0])
    pieces = [slice(lo, hi) for lo, hi in zip(cuts, cuts[1:])]
    copies = [
        pltpu.make_async_copy(weight.at[p], weight_v.at[p], sems.at[1 + k]) for k, p in enumerate(pieces)
    ]
    for copy in [own, *copies]:
        copy.start()
    own.wait()
    raws = [0.0] * blocks
    for p, copy in zip(pieces, copies):
        copy.wait()
        for b in range(blocks):
            left = own_v[:, p] if b == 0 else feats[b][:, p]
            raws[b] = raws[b] + dot(left, weight_v[p])
    embs[0][...], inverse[...] = normalised(raws[0])
    for b in range(1, blocks):
        embs[b][...] = normalised(raws[b])[0]


def stream_embed(feats, weight, keep):
    (rows, depth), blocks = feats[0].shape, len(feats)
    cuts = [depth // LANES * k // PIECES * LANES for k in range(PIECES)] + [depth]
    far = [pltpu.with_memory_space_constraint(a, pltpu.HBM) for a in (feats[0], weight)]
    near = [pltpu.with_memory_space_constraint(a, pltpu.VMEM) for a in feats[1:]]
    hbm, vmem = pl.BlockSpec(memory_space=pltpu.HBM), pl.BlockSpec(memory_space=pltpu.VMEM)
    outs = [((rows, weight.shape[1]), BF16)] * blocks + [((rows, 1), F32)] + [(weight.shape, BF16)] * keep
    out = pl.pallas_call(
        functools.partial(stream_kernel, blocks, cuts),
        out_shape=[jax.ShapeDtypeStruct(*o) for o in outs],
        in_specs=[hbm] + [vmem] * (blocks - 1) + [hbm],
        out_specs=[vmem] * len(outs),
        scratch_shapes=[pltpu.VMEM(weight.shape, BF16)] * (not keep)
        + [pltpu.VMEM((rows, depth), BF16), pltpu.SemaphoreType.DMA((PIECES + 1,))],
        compiler_params=pltpu.CompilerParams(vmem_limit_bytes=16 << 20),
        cost_estimate=pl.CostEstimate(
            flops=2 * blocks * rows * weight.size, bytes_accessed=2 * weight.size, transcendentals=0
        ),
    )(far[0], *near, far[1])
    return list(out[:blocks]), *out[blocks:]


def keys_kernel(*refs):
    for feats, factor, inverse, wide in zip(refs[:2], refs[2:4], refs[4:6], refs[6:8]):
        keys = dot(feats[...], factor[...], 1, 1) * inverse[...]
        for a in range(keys.shape[1]):
            wide[:, a * LANES : (a + 1) * LANES] = jnp.broadcast_to(keys[:, a : a + 1], (keys.shape[0], LANES))


def hold(x, after):
    args = [pltpu.with_memory_space_constraint(a, pltpu.VMEM) for a in [x, *after]]
    return pl.pallas_call(
        lambda *refs: None,
        out_shape=jax.ShapeDtypeStruct(x.shape, x.dtype),
        in_specs=[pl.BlockSpec(memory_space=pltpu.VMEM)] * len(args),
        out_specs=pl.BlockSpec(memory_space=pltpu.VMEM),
        input_output_aliases={0: 0},
        compiler_params=pltpu.CompilerParams(vmem_limit_bytes=1 << 20),
    )(*args)


def column_of(row):
    return jnp.broadcast_to(row, (LANES, LANES)).T


def scores_kernel(ni, nt, *refs):
    images, texts = refs[:ni], refs[ni : ni + nt]
    raw, row_lse, col_lse, all_images, all_texts = refs[ni + nt :]
    rows = images[0].shape[0]
    for a in range(ni):
        all_images[a * rows : (a + 1) * rows] = images[a][...]
    for t in range(nt):
        all_texts[t * rows : (t + 1) * rows] = texts[t][...]
    raw[...] = dot(all_images[...], all_texts[...], 1, 1)
    for a in range(ni):
        scores = LOGIT_SCALE * raw[a * rows : (a + 1) * rows]
        top = jnp.max(scores, axis=1, keepdims=True)
        lse = top + jnp.log(jnp.sum(jnp.exp(scores - top), axis=1, keepdims=True))
        row_lse[a : a + 1] = jnp.broadcast_to(lse, (rows, LANES)).T[:1]
    for t in range(nt):
        scores = LOGIT_SCALE * raw[:, t * rows : (t + 1) * rows]
        top = jnp.max(scores, axis=0, keepdims=True)
        col_lse[t : t + 1] = top + jnp.log(jnp.sum(jnp.exp(scores - top), axis=0, keepdims=True))


def factors_kernel(ni, nt, *refs):
    images, texts, (b_img, b_txt) = refs[:ni], refs[ni : ni + nt], refs[ni + nt : ni + nt + 2]
    img_low, img_side_t, txt_low, txt_side_t, img_base, txt_base = refs[ni + nt + 2 :]
    rows = images[0].shape[0]
    for a in range(ni):
        here = slice(a * rows, (a + 1) * rows)
        low = dot(images[a][...], b_img[...])
        side = dot(images[a][...], b_txt[...])
        img_low[here] = low
        img_side_t[:, here] = side.T.astype(BF16)
        if a == 0:
            own_img_low, own_img_side = low, side.astype(BF16).astype(F32)
    for t in range(nt):
        here = slice(t * rows, (t + 1) * rows)
        low = dot(texts[t][...], b_img[...]).astype(BF16)
        side = dot(texts[t][...], b_txt[...])
        txt_low[here] = low
        txt_side_t[:, here] = side.T
        if t == 0:
            own_txt_low, own_txt_side = low.astype(F32), side
    diagonal = jnp.sum(
        images[0][...].astype(F32) * texts[0][...].astype(F32), axis=1, keepdims=True
    )
    img_base[...] = 2.0 * (diagonal * own_img_low - own_txt_low)
    txt_base[...] = 2.0 * (diagonal * own_txt_side - own_img_side)


def merge(parts):
    slots = parts[0].shape[0]
    lined = [parts[0][...]]
    for k in range(1, len(parts)):
        lined.append(
            jnp.concatenate([parts[k][s ^ k : (s ^ k) + 1] for s in range(slots)], axis=0)
        )
    top = functools.reduce(jnp.maximum, lined)
    return top + jnp.log(sum(jnp.exp(p - top) for p in lined))


def add_kernel(count, *refs):
    own, got, sent = refs[:count], refs[count:-1], refs[-1]
    rows = own[0].shape[0]
    for k in range(count):
        part = own[k][...]
        for arrived in got:
            at = (count + k) * rows
            part = part + arrived[at : at + rows].astype(F32)
        sent[k * rows : (k + 1) * rows] = part.astype(sent.dtype)


def halve(kept, sent, bits, n):
    rows = kept[0].shape[0]
    got = [swap(sent, bits[-1], n)]
    for bit in bits[-2::-1]:
        upper = kept[len(kept) // 2 :]
        (sent,) = call(
            functools.partial(add_kernel, len(upper)),
            [((len(upper) * rows, kept[0].shape[1]), BF16)],
            [*upper, *got],
        )
        kept = kept[: len(kept) // 2]
        got.append(swap(sent, bit, n))
    return [kept[0], *got], sent


def weights_kernel(ni, nt, *refs):
    row_parts, col_parts = refs[:ni], refs[ni : ni + nt]
    raw, img_low, img_side_t, txt_low, txt_side_t = refs[ni + nt : ni + nt + 5]
    half = ni // 2
    img_kept, img_sent = refs[ni + nt + 5 : ni + nt + 5 + half], refs[ni + nt + 5 + half]
    txt_parts, weights_bf = refs[-1 - nt : -1], refs[-1]
    rows = LANES
    row_lse = merge(row_parts)
    col_lse = merge(col_parts)
    inner_col = [jnp.zeros((1, rows), F32) for _ in range(nt)]
    for a in range(ni):
        row = column_of(row_lse[a : a + 1])
        inner_row = jnp.zeros((rows, rows), F32)
        for t in range(nt):
            here = raw[a * rows : (a + 1) * rows, t * rows : (t + 1) * rows]
            scores = LOGIT_SCALE * here
            weights = jnp.exp(scores - row) + jnp.exp(scores - col_lse[t : t + 1])
            weights_bf[a * rows : (a + 1) * rows, t * rows : (t + 1) * rows] = weights.astype(BF16)
            weighted = weights * here
            inner_row = inner_row + weighted
            inner_col[t] = inner_col[t] + jnp.sum(weighted, axis=0, keepdims=True)
        inner = jnp.sum(inner_row, axis=1, keepdims=True)
        part = (
            dot(weights_bf[a * rows : (a + 1) * rows], txt_low[...])
            - inner * img_low[a * rows : (a + 1) * rows]
        )
        if a < half:
            img_kept[a][...] = part
        else:
            img_sent[(a - half) * rows : (a - half + 1) * rows] = part.astype(img_sent.dtype)
    for t in range(nt):
        here = slice(t * rows, (t + 1) * rows)
        part = dot(img_side_t[...], weights_bf[:, here]) - inner_col[t] * txt_side_t[:, here]
        txt_parts[t][...] = part.astype(txt_parts[t].dtype)


def sketch_kernel(count, turned, *refs):
    parts, (base, keys, out, made, sems) = refs[:count], refs[count:]
    rows = base.shape[0]
    grad = sum((part[:rows].astype(F32) for part in parts[1:]), parts[0][...])
    grad = (grad.T if turned else grad) + base[...]
    copies, step = [], rows // 2
    for k in range(2):
        here = slice(k * step, (k + 1) * step)
        for a in range(0, made.shape[1], LANES):
            made[here, a : a + LANES] = (keys[here, a : a + LANES] * grad[here]).astype(BF16)
        copies.append(pltpu.make_async_copy(made.at[here], out.at[here], sems.at[k]))
        copies[-1].start()
    for copy in copies:
        copy.wait()


def sketch(parts, base, keys, turned):
    args = [pltpu.with_memory_space_constraint(a, pltpu.VMEM) for a in [*parts, base, keys]]
    return pl.pallas_call(
        functools.partial(sketch_kernel, len(parts), turned),
        out_shape=jax.ShapeDtypeStruct(keys.shape, BF16),
        in_specs=[pl.BlockSpec(memory_space=pltpu.VMEM)] * len(args),
        out_specs=pl.BlockSpec(memory_space=pltpu.HBM),
        scratch_shapes=[pltpu.VMEM(keys.shape, BF16), pltpu.SemaphoreType.DMA((2,))],
        compiler_params=pltpu.CompilerParams(vmem_limit_bytes=16 << 20),
        cost_estimate=pl.CostEstimate(flops=keys.size, bytes_accessed=6 * keys.size, transcendentals=0),
    )(*args)


def body(n, img_feats, txt_feats, w_img, w_txt, a_img, b_img, a_txt, b_txt):
    rows, wide = img_feats.shape[0], w_img.shape[1]
    low = b_img.shape[1]
    assert rows == LANES and low == LANES
    img_bits, txt_bits = split_bits(n)
    img_span, txt_span = span(img_bits), span(txt_bits)
    ni, nt = len(img_span), len(txt_span)
    (img_emb,), img_inv = stream_embed([img_feats], w_img, False)
    feats = gather(txt_feats, txt_bits, n)
    texts, txt_inv, w_txt_v = stream_embed(feats[:-1], w_txt, True)
    img_keys, txt_keys = call(
        keys_kernel,
        [((rows, a_img.shape[1] * LANES), F32), ((rows, a_txt.shape[1] * LANES), F32)],
        [img_feats, txt_feats, a_img.T, a_txt.T, img_inv, txt_inv],
    )
    images = gather(img_emb, img_bits, n, lambda x: hold(x, [texts[0], img_keys]))
    texts = texts + embed(feats[-1:], w_txt_v)
    raw, row_lse, col_lse = call(
        functools.partial(scores_kernel, ni, nt),
        [((ni * rows, nt * rows), F32), ((ni, rows), F32), ((nt, rows), F32)],
        images + texts,
        scratch=[pltpu.VMEM((ni * rows, wide), BF16), pltpu.VMEM((nt * rows, wide), BF16)],
        flops=2 * ni * nt * rows * rows * wide,
    )
    row_parts = gather(row_lse, img_bits, n)
    col_parts = [col_lse] + [swap(col_lse, o, n) for o in txt_span[1:]]
    img_low, img_side_t, txt_low, txt_side_t, img_base, txt_base = call(
        functools.partial(factors_kernel, ni, nt),
        [
            ((ni * rows, low), F32),
            ((low, ni * rows), BF16),
            ((nt * rows, low), BF16),
            ((low, nt * rows), F32),
            ((rows, low), F32),
            ((rows, low), F32),
        ],
        images + texts + [b_img, b_txt],
        flops=4 * (ni + nt) * rows * wide * low,
    )
    half = ni // 2
    parts = call(
        functools.partial(weights_kernel, ni, nt),
        [((rows, low), F32)] * half
        + [((half * rows, low), BF16), ((rows, low), F32)]
        + [((rows, low), BF16)] * (nt - 1),
        row_parts + col_parts + [raw, img_low, img_side_t, txt_low, txt_side_t],
        scratch=[pltpu.VMEM((ni * rows, nt * rows), BF16)],
        flops=4 * ni * nt * rows * rows * low,
    )
    img_parts, last = halve(list(parts[:half]), parts[half], img_bits, n)
    txt_parts = list(parts[half + 1 :])
    txt_parts[2:] = [hold(p, [last]) for p in txt_parts[2:]]
    txt_parts = txt_parts[:1] + [swap(p, o, n) for p, o in zip(txt_parts[1:], txt_span[1:])]
    return (
        sketch(img_parts, img_base, img_keys, False),
        sketch(txt_parts, txt_base, txt_keys, True),
    )


def solution(mesh):
    n = mesh.shape["dp"]
    rows = P(("ckpt", "dp"), None)
    part = P("ckpt", None)
    return jax.shard_map(
        lambda *args: body(n, *args),
        mesh=mesh,
        in_specs=(rows, rows, part, part, P(), P(), P(), P()),
        out_specs=(rows, rows),
        check_vma=False,
    )
```

```python
import functools
import jax
import jax.numpy as jnp
from jax import lax
from jax.experimental import pallas as pl
from jax.experimental.pallas import tpu as pltpu
from jax.sharding import PartitionSpec as P

LOGIT_SCALE = 100.0
EPSILON = 1e-06
F32 = jnp.float32
BF16 = jnp.bfloat16
LANES = 128
PIECES = 4


def dot(left, right, left_dim=1, right_dim=0):
    return lax.dot_general(
        left, right, (((left_dim,), (right_dim,)), ((), ())), preferred_element_type=F32
    )


def skip(kernel, first, count, *refs):
    kernel(*refs[:first], *refs[first + count :])


def call(kernel, outs, args, after=(), free=(), scratch=(), flops=0, limit=16):
    args = [a if k in free else pltpu.with_memory_space_constraint(a, pltpu.VMEM) for k, a in enumerate(args)]
    size = sum(a.size * a.dtype.itemsize for a in args)
    specs = [pl.BlockSpec(memory_space=pltpu.VMEM)] * len(args)
    if after:
        kernel = functools.partial(skip, kernel, len(args), len(after))
        args, specs = args + list(after), specs + [pl.BlockSpec(memory_space=pl.ANY)] * len(after)
    return pl.pallas_call(
        kernel,
        out_shape=[jax.ShapeDtypeStruct(s, d) for s, d in outs],
        in_specs=specs,
        out_specs=[pl.BlockSpec(memory_space=pltpu.VMEM)] * len(outs),
        scratch_shapes=list(scratch),
        compiler_params=pltpu.CompilerParams(vmem_limit_bytes=limit << 20),
        cost_estimate=pl.CostEstimate(flops=flops, bytes_accessed=size, transcendentals=0),
    )(*args)


def span(bits):
    offsets = [0]
    for bit in bits:
        offsets = offsets + [o ^ bit for o in offsets]
    return offsets


def split_bits(n):
    bits = [1 << b for b in range(n.bit_length() - 1)]
    assert 1 << len(bits) == n
    half = len(bits) // 2
    return bits[:half:-1] + bits[:1], bits[half:0:-1]


def swap(x, offset, n):
    return lax.ppermute(x, "dp", [(i, i ^ offset) for i in range(n)])


def gather(block, bits, n, ready=lambda x: x):
    blocks, sent = [block], [block]
    for bit in bits:
        new = [swap(b, bit, n) for b in sent]
        blocks, sent = blocks + new, sent + [ready(b) for b in new]
    return blocks


def normalised(raw):
    inverse = lax.rsqrt(jnp.sum(raw * raw, axis=1, keepdims=True) + EPSILON)
    return (raw * inverse).astype(BF16), inverse


def embed_kernel(blocks, *refs):
    feats, weight, embs = refs[:blocks], refs[blocks], refs[blocks + 1 :]
    for b in range(blocks):
        embs[b][...] = normalised(dot(feats[b][...], weight[...]))[0]


def embed(feats, weight):
    rows, blocks = feats[0].shape[0], len(feats)
    return list(
        call(
            functools.partial(embed_kernel, blocks),
            [((rows, weight.shape[1]), BF16)] * blocks,
            [*feats, weight],
            flops=2 * blocks * rows * weight.size,
        )
    )


def stream_kernel(blocks, cuts, *refs):
    feats, weight, embs = refs[:blocks], refs[blocks], refs[blocks + 1 : 2 * blocks + 1]
    inverse, weight_v, own_v, sems = refs[2 * blocks + 1 :]
    own = pltpu.make_async_copy(feats[0], own_v, sems.at[0])
    pieces = [slice(lo, hi) for lo, hi in zip(cuts, cuts[1:])]
    copies = [
        pltpu.make_async_copy(weight.at[p], weight_v.at[p], sems.at[1 + k]) for k, p in enumerate(pieces)
    ]
    for copy in [own, *copies]:
        copy.start()
    own.wait()
    raws = [0.0] * blocks
    for p, copy in zip(pieces, copies):
        copy.wait()
        for b in range(blocks):
            left = own_v[:, p] if b == 0 else feats[b][:, p]
            raws[b] = raws[b] + dot(left, weight_v[p])
    embs[0][...], inverse[...] = normalised(raws[0])
    for b in range(1, blocks):
        embs[b][...] = normalised(raws[b])[0]


def stream_embed(feats, weight, keep):
    (rows, depth), blocks = feats[0].shape, len(feats)
    cuts = [depth // LANES * k // PIECES * LANES for k in range(PIECES)] + [depth]
    far = [pltpu.with_memory_space_constraint(a, pltpu.HBM) for a in (feats[0], weight)]
    near = [pltpu.with_memory_space_constraint(a, pltpu.VMEM) for a in feats[1:]]
    hbm, vmem = pl.BlockSpec(memory_space=pltpu.HBM), pl.BlockSpec(memory_space=pltpu.VMEM)
    outs = [((rows, weight.shape[1]), BF16)] * blocks + [((rows, 1), F32)] + [(weight.shape, BF16)] * keep
    out = pl.pallas_call(
        functools.partial(stream_kernel, blocks, cuts),
        out_shape=[jax.ShapeDtypeStruct(*o) for o in outs],
        in_specs=[hbm] + [vmem] * (blocks - 1) + [hbm],
        out_specs=[vmem] * len(outs),
        scratch_shapes=[pltpu.VMEM(weight.shape, BF16)] * (not keep)
        + [pltpu.VMEM((rows, depth), BF16), pltpu.SemaphoreType.DMA((PIECES + 1,))],
        compiler_params=pltpu.CompilerParams(vmem_limit_bytes=16 << 20),
        cost_estimate=pl.CostEstimate(
            flops=2 * blocks * rows * weight.size, bytes_accessed=2 * weight.size, transcendentals=0
        ),
    )(far[0], *near, far[1])
    return list(out[:blocks]), *out[blocks:]


def keys_kernel(*refs):
    for feats, factor, inverse, wide in zip(refs[:2], refs[2:4], refs[4:6], refs[6:8]):
        keys = dot(feats[...], factor[...], 1, 1) * inverse[...]
        for a in range(keys.shape[1]):
            wide[:, a * LANES : (a + 1) * LANES] = jnp.broadcast_to(keys[:, a : a + 1], (keys.shape[0], LANES))


def hold(x, after):
    args = [pltpu.with_memory_space_constraint(a, pltpu.VMEM) for a in [x, *after]]
    return pl.pallas_call(
        lambda *refs: None,
        out_shape=jax.ShapeDtypeStruct(x.shape, x.dtype),
        in_specs=[pl.BlockSpec(memory_space=pltpu.VMEM)] * len(args),
        out_specs=pl.BlockSpec(memory_space=pltpu.VMEM),
        input_output_aliases={0: 0},
        compiler_params=pltpu.CompilerParams(vmem_limit_bytes=1 << 20),
    )(*args)


def column_of(row):
    return jnp.broadcast_to(row, (LANES, LANES)).T


def lse_parts(scores, axis):
    top = jnp.max(scores, axis=axis, keepdims=True)
    return top, jnp.sum(jnp.exp(scores - top), axis=axis, keepdims=True)


def scores_kernel(ni, nt, *refs):
    images, texts = refs[:ni], refs[ni : ni + nt]
    raw, row_lse, col_top, col_total, all_images, all_texts = refs[ni + nt :]
    rows = images[0].shape[0]
    for a in range(ni):
        all_images[a * rows : (a + 1) * rows] = images[a][...]
    for t in range(nt):
        all_texts[t * rows : (t + 1) * rows] = texts[t][...]
    raw[...] = dot(all_images[...], all_texts[...], 1, 1)
    for a in range(ni):
        top, total = lse_parts(LOGIT_SCALE * raw[a * rows : (a + 1) * rows], 1)
        row_lse[a : a + 1] = jnp.broadcast_to(top + jnp.log(total), (rows, LANES)).T[:1]
    for t in range(nt):
        col_top[t : t + 1], col_total[t : t + 1] = lse_parts(LOGIT_SCALE * raw[:, t * rows : (t + 1) * rows], 0)


def last_scores_kernel(ni, nt, *refs):
    image, texts, (rows_lse, tops, totals) = refs[0], refs[1 : 1 + nt], refs[1 + nt : 4 + nt]
    raw, row_lse, col_lse, all_texts = refs[4 + nt :]
    rows = image.shape[0]
    for t in range(nt):
        all_texts[t * rows : (t + 1) * rows] = texts[t][...]
    raw[...] = dot(image[...], all_texts[...], 1, 1)
    top, total = lse_parts(LOGIT_SCALE * raw[...], 1)
    row_lse[: ni - 1] = rows_lse[...]
    row_lse[ni - 1 :] = jnp.broadcast_to(top + jnp.log(total), (rows, LANES)).T[:1]
    for t in range(nt):
        top, total = lse_parts(LOGIT_SCALE * raw[:, t * rows : (t + 1) * rows], 0)
        high = jnp.maximum(top, tops[t : t + 1])
        total = total * jnp.exp(top - high) + totals[t : t + 1] * jnp.exp(tops[t : t + 1] - high)
        col_lse[t : t + 1] = high + jnp.log(total)


def factors_kernel(ni, nt, *refs):
    images, texts, (b_img, b_txt) = refs[:ni], refs[ni : ni + nt], refs[ni + nt : ni + nt + 2]
    img_low, img_side_t, txt_low, txt_side_t, img_base, txt_base = refs[ni + nt + 2 :]
    rows = images[0].shape[0]
    for a in range(ni):
        here = slice(a * rows, (a + 1) * rows)
        low = dot(images[a][...], b_img[...])
        side = dot(images[a][...], b_txt[...])
        img_low[here] = low
        img_side_t[:, here] = side.T.astype(BF16)
        if a == 0:
            own_img_low, own_img_side = low, side.astype(BF16).astype(F32)
    for t in range(nt):
        here = slice(t * rows, (t + 1) * rows)
        low = dot(texts[t][...], b_img[...]).astype(BF16)
        side = dot(texts[t][...], b_txt[...])
        txt_low[here] = low
        txt_side_t[:, here] = side.T
        if t == 0:
            own_txt_low, own_txt_side = low.astype(F32), side
    diagonal = jnp.sum(
        images[0][...].astype(F32) * texts[0][...].astype(F32), axis=1, keepdims=True
    )
    img_base[...] = 2.0 * (diagonal * own_img_low - own_txt_low)
    txt_base[...] = 2.0 * (diagonal * own_txt_side - own_img_side)


def merge(parts, flips):
    slots = parts[0].shape[0]
    lined = [parts[0][...]]
    for k in range(1, len(parts)):
        lined.append(
            jnp.concatenate([parts[k][s ^ flips[k] :][:1] for s in range(slots)], axis=0)
        )
    top = functools.reduce(jnp.maximum, lined)
    return top + jnp.log(sum(jnp.exp(p - top) for p in lined))


def merge_kernel(flips, *refs):
    refs[-1][...] = merge(refs[:-1], flips)


def gather_lse(lse, bits, n):
    for j, bit in enumerate(bits[:-1]):
        (lse,) = call(functools.partial(merge_kernel, (0, 1 << j)), [(lse.shape, F32)], [lse, swap(lse, bit, n)])
    return [lse, swap(lse, bits[-1], n)], (0, 1 << len(bits) - 1)


def add_kernel(count, *refs):
    own, got, sent = refs[:count], refs[count:-1], refs[-1]
    rows = own[0].shape[0]
    for k in range(count):
        part = own[k][...]
        for arrived in got:
            at = (count + k) * rows
            part = part + arrived[at : at + rows].astype(F32)
        sent[k * rows : (k + 1) * rows] = part.astype(sent.dtype)


def halve(kept, sent, bits, n):
    rows = kept[0].shape[0]
    got = [swap(sent, bits[-1], n)]
    for bit in bits[-2::-1]:
        upper = kept[len(kept) // 2 :]
        (sent,) = call(
            functools.partial(add_kernel, len(upper)),
            [((len(upper) * rows, kept[0].shape[1]), BF16)],
            [*upper, *got],
        )
        kept = kept[: len(kept) // 2]
        got.append(swap(sent, bit, n))
    return [kept[0], *got], sent


def weights_kernel(ni, nt, row_flips, col_flips, *refs):
    row_parts, refs = refs[: len(row_flips)], refs[len(row_flips) :]
    col_parts, refs = refs[: len(col_flips)], refs[len(col_flips) :]
    raw, last_raw, img_low, txt_low = refs[:4]
    half = ni // 2
    *img_kept, img_sent, weights_bf, inners = refs[4:]
    rows = LANES
    row_lse = merge(row_parts, row_flips)
    col_lse = merge(col_parts, col_flips)
    inner_col = [jnp.zeros((1, rows), F32) for _ in range(nt)]
    for a in range(ni):
        row = column_of(row_lse[a : a + 1])
        inner_row = jnp.zeros((rows, rows), F32)
        for t in range(nt):
            cols = slice(t * rows, (t + 1) * rows)
            here = raw[a * rows : (a + 1) * rows, cols] if a < ni - 1 else last_raw[:, cols]
            scores = LOGIT_SCALE * here
            weights = jnp.exp(scores - row) + jnp.exp(scores - col_lse[t : t + 1])
            weights_bf[a * rows : (a + 1) * rows, t * rows : (t + 1) * rows] = weights.astype(BF16)
            weighted = weights * here
            inner_row = inner_row + weighted
            inner_col[t] = inner_col[t] + jnp.sum(weighted, axis=0, keepdims=True)
        inner = jnp.sum(inner_row, axis=1, keepdims=True)
        part = (
            dot(weights_bf[a * rows : (a + 1) * rows], txt_low[...])
            - inner * img_low[a * rows : (a + 1) * rows]
        )
        if a < half:
            img_kept[a][...] = part
        else:
            img_sent[(a - half) * rows : (a - half + 1) * rows] = part.astype(img_sent.dtype)
    for t in range(nt):
        inners[t : t + 1] = inner_col[t]


def columns_kernel(nt, weights_bf, inners, img_side_t, txt_side_t, *refs):
    rows, kept, sent = LANES, refs[:-1], refs[-1]
    for t in range(nt):
        here = slice(t * rows, (t + 1) * rows)
        part = dot(img_side_t[...], weights_bf[:, here]) - inners[t : t + 1] * txt_side_t[:, here]
        if t < nt // 2:
            kept[t][...] = part
        else:
            sent[(t - nt // 2) * rows : (t - nt // 2 + 1) * rows] = part.astype(sent.dtype)


def sketch_kernel(count, turned, *refs):
    parts, (base, keys, out, made, sems) = refs[:count], refs[count:]
    rows = base.shape[0]
    grad = sum((part[:rows].astype(F32) for part in parts[1:]), parts[0][...])
    grad = (grad.T if turned else grad) + base[...]
    copies, step = [], rows // 2
    for k in range(2):
        here = slice(k * step, (k + 1) * step)
        for a in range(0, made.shape[1], LANES):
            made[here, a : a + LANES] = (keys[here, a : a + LANES] * grad[here]).astype(BF16)
        copies.append(pltpu.make_async_copy(made.at[here], out.at[here], sems.at[k]))
        copies[-1].start()
    for copy in copies:
        copy.wait()


def sketch(parts, base, keys, turned):
    args = [pltpu.with_memory_space_constraint(a, pltpu.VMEM) for a in [*parts, base, keys]]
    return pl.pallas_call(
        functools.partial(sketch_kernel, len(parts), turned),
        out_shape=jax.ShapeDtypeStruct(keys.shape, BF16),
        in_specs=[pl.BlockSpec(memory_space=pltpu.VMEM)] * len(args),
        out_specs=pl.BlockSpec(memory_space=pltpu.HBM),
        scratch_shapes=[pltpu.VMEM(keys.shape, BF16), pltpu.SemaphoreType.DMA((2,))],
        compiler_params=pltpu.CompilerParams(vmem_limit_bytes=16 << 20),
        cost_estimate=pl.CostEstimate(flops=keys.size, bytes_accessed=6 * keys.size, transcendentals=0),
    )(*args)


def body(n, img_feats, txt_feats, w_img, w_txt, a_img, b_img, a_txt, b_txt):
    rows, wide = img_feats.shape[0], w_img.shape[1]
    low = b_img.shape[1]
    assert rows == LANES and low == LANES
    img_bits, txt_bits = split_bits(n)
    img_span, txt_span = span(img_bits), span(txt_bits)
    ni, nt = len(img_span), len(txt_span)
    (img_emb,), img_inv = stream_embed([img_feats], w_img, False)
    feats = gather(txt_feats, txt_bits, n)
    texts, txt_inv, w_txt_v = stream_embed(feats[:-1], w_txt, True)
    img_keys, txt_keys = call(
        keys_kernel,
        [((rows, a_img.shape[1] * LANES), F32), ((rows, a_txt.shape[1] * LANES), F32)],
        [img_feats, txt_feats, a_img.T, a_txt.T, img_inv, txt_inv],
    )
    images = gather(img_emb, img_bits, n, lambda x: hold(x, [texts[0], img_keys]))
    texts = texts + embed(feats[-1:], w_txt_v)
    raw, rows_lse, tops, totals = call(
        functools.partial(scores_kernel, ni - 1, nt),
        [(((ni - 1) * rows, nt * rows), F32), ((ni - 1, rows), F32), ((nt, rows), F32), ((nt, rows), F32)],
        images[:-1] + texts,
        scratch=[pltpu.VMEM(((ni - 1) * rows, wide), BF16), pltpu.VMEM((nt * rows, wide), BF16)],
        flops=2 * (ni - 1) * nt * rows * rows * wide,
    )
    last_raw, row_lse, col_lse = call(
        functools.partial(last_scores_kernel, ni, nt),
        [((rows, nt * rows), F32), ((ni, rows), F32), ((nt, rows), F32)],
        images[-1:] + texts + [rows_lse, tops, totals],
        scratch=[pltpu.VMEM((nt * rows, wide), BF16)],
        flops=2 * nt * rows * rows * wide,
    )
    row_parts = gather(row_lse, img_bits, n)
    col_parts, col_flips = gather_lse(col_lse, txt_bits, n)
    img_low, img_side_t, txt_low, txt_side_t, img_base, txt_base = call(
        functools.partial(factors_kernel, ni, nt),
        [
            ((ni * rows, low), F32),
            ((low, ni * rows), BF16),
            ((nt * rows, low), BF16),
            ((low, nt * rows), F32),
            ((rows, low), F32),
            ((rows, low), F32),
        ],
        images + texts + [b_img, b_txt],
        flops=4 * (ni + nt) * rows * wide * low,
    )
    half = ni // 2
    *img_kept, img_sent, weights_bf, inners = call(
        functools.partial(weights_kernel, ni, nt, tuple(range(ni)), col_flips),
        [((rows, low), F32)] * half
        + [((half * rows, low), BF16), ((ni * rows, nt * rows), BF16), ((nt, rows), F32)],
        row_parts + col_parts + [raw, last_raw, img_low, txt_low],
        flops=2 * ni * nt * rows * rows * low,
    )
    *txt_kept, txt_sent = call(
        functools.partial(columns_kernel, nt),
        [((rows, low), F32)] * (nt // 2) + [((nt // 2 * rows, low), BF16)],
        [weights_bf, inners, img_side_t, txt_side_t],
        flops=2 * ni * nt * rows * rows * low,
    )
    img_parts, _ = halve(img_kept, img_sent, img_bits, n)
    txt_parts, _ = halve(txt_kept, txt_sent, txt_bits, n)
    return (
        sketch(img_parts, img_base, img_keys, False),
        sketch(txt_parts, txt_base, txt_keys, True),
    )


def solution(mesh):
    n = mesh.shape["dp"]
    rows = P(("ckpt", "dp"), None)
    part = P("ckpt", None)
    return jax.shard_map(
        lambda *args: body(n, *args),
        mesh=mesh,
        in_specs=(rows, rows, part, part, P(), P(), P(), P()),
        out_specs=(rows, rows),
        check_vma=False,
    )
```

```python
import functools
import jax
import jax.numpy as jnp
from jax import lax
from jax.experimental import pallas as pl
from jax.experimental.pallas import tpu as pltpu
from jax.sharding import PartitionSpec as P

LOGIT_SCALE = 100.0
EPSILON = 1e-06
F32 = jnp.float32
BF16 = jnp.bfloat16
LANES = 128
PIECES = 4


def dot(left, right, left_dim=1, right_dim=0):
    return lax.dot_general(
        left, right, (((left_dim,), (right_dim,)), ((), ())), preferred_element_type=F32
    )


def skip(kernel, first, count, *refs):
    kernel(*refs[:first], *refs[first + count :])


def call(kernel, outs, args, after=(), free=(), scratch=(), flops=0, limit=16):
    args = [a if k in free else pltpu.with_memory_space_constraint(a, pltpu.VMEM) for k, a in enumerate(args)]
    size = sum(a.size * a.dtype.itemsize for a in args)
    specs = [pl.BlockSpec(memory_space=pltpu.VMEM)] * len(args)
    if after:
        kernel = functools.partial(skip, kernel, len(args), len(after))
        args, specs = args + list(after), specs + [pl.BlockSpec(memory_space=pl.ANY)] * len(after)
    return pl.pallas_call(
        kernel,
        out_shape=[jax.ShapeDtypeStruct(s, d) for s, d in outs],
        in_specs=specs,
        out_specs=[pl.BlockSpec(memory_space=pltpu.VMEM)] * len(outs),
        scratch_shapes=list(scratch),
        compiler_params=pltpu.CompilerParams(vmem_limit_bytes=limit << 20),
        cost_estimate=pl.CostEstimate(flops=flops, bytes_accessed=size, transcendentals=0),
    )(*args)


def span(bits):
    offsets = [0]
    for bit in bits:
        offsets = offsets + [o ^ bit for o in offsets]
    return offsets


def split_bits(n):
    bits = [1 << b for b in range(n.bit_length() - 1)]
    assert 1 << len(bits) == n
    half = len(bits) // 2
    return bits[:half:-1] + bits[:1], bits[half:0:-1]


def swap(x, offset, n):
    return lax.ppermute(x, "dp", [(i, i ^ offset) for i in range(n)])


def gather(block, bits, n, ready=None):
    blocks = [block]
    for bit in bits:
        new = [swap(b, bit, n) for b in blocks]
        blocks = blocks + (new if ready is None or bit == bits[-1] else [ready(b) for b in new])
    return blocks


def normalised(raw):
    inverse = lax.rsqrt(jnp.sum(raw * raw, axis=1, keepdims=True) + EPSILON)
    return (raw * inverse).astype(BF16), inverse


def embed_kernel(blocks, *refs):
    feats, weight, embs = refs[:blocks], refs[blocks], refs[blocks + 1 :]
    for b in range(blocks):
        embs[b][...] = normalised(dot(feats[b][...], weight[...]))[0]


def embed(feats, weight):
    rows, blocks = feats[0].shape[0], len(feats)
    return list(
        call(
            functools.partial(embed_kernel, blocks),
            [((rows, weight.shape[1]), BF16)] * blocks,
            [*feats, weight],
            flops=2 * blocks * rows * weight.size,
        )
    )


def stream_kernel(blocks, cuts, *refs):
    feats, weight, embs = refs[:blocks], refs[blocks], refs[blocks + 1 : 2 * blocks + 1]
    inverse, weight_v, own_v, sems = refs[2 * blocks + 1 :]
    own = pltpu.make_async_copy(feats[0], own_v, sems.at[0])
    pieces = [slice(lo, hi) for lo, hi in zip(cuts, cuts[1:])]
    copies = [
        pltpu.make_async_copy(weight.at[p], weight_v.at[p], sems.at[1 + k]) for k, p in enumerate(pieces)
    ]
    for copy in [own, *copies]:
        copy.start()
    own.wait()
    raws = [0.0] * blocks
    for p, copy in zip(pieces, copies):
        copy.wait()
        for b in range(blocks):
            left = own_v[:, p] if b == 0 else feats[b][:, p]
            raws[b] = raws[b] + dot(left, weight_v[p])
    embs[0][...], inverse[...] = normalised(raws[0])
    for b in range(1, blocks):
        embs[b][...] = normalised(raws[b])[0]


def stream_embed(feats, weight, keep):
    (rows, depth), blocks = feats[0].shape, len(feats)
    cuts = [depth // LANES * k // PIECES * LANES for k in range(PIECES)] + [depth]
    far = [pltpu.with_memory_space_constraint(a, pltpu.HBM) for a in (feats[0], weight)]
    near = [pltpu.with_memory_space_constraint(a, pltpu.VMEM) for a in feats[1:]]
    hbm, vmem = pl.BlockSpec(memory_space=pltpu.HBM), pl.BlockSpec(memory_space=pltpu.VMEM)
    outs = [((rows, weight.shape[1]), BF16)] * blocks + [((rows, 1), F32)] + [(weight.shape, BF16)] * keep
    out = pl.pallas_call(
        functools.partial(stream_kernel, blocks, cuts),
        out_shape=[jax.ShapeDtypeStruct(*o) for o in outs],
        in_specs=[hbm] + [vmem] * (blocks - 1) + [hbm],
        out_specs=[vmem] * len(outs),
        scratch_shapes=[pltpu.VMEM(weight.shape, BF16)] * (not keep)
        + [pltpu.VMEM((rows, depth), BF16), pltpu.SemaphoreType.DMA((PIECES + 1,))],
        compiler_params=pltpu.CompilerParams(vmem_limit_bytes=16 << 20),
        cost_estimate=pl.CostEstimate(
            flops=2 * blocks * rows * weight.size, bytes_accessed=2 * weight.size, transcendentals=0
        ),
    )(far[0], *near, far[1])
    return list(out[:blocks]), *out[blocks:]


def keys_kernel(*refs):
    for feats, factor, inverse, wide in zip(refs[:2], refs[2:4], refs[4:6], refs[6:8]):
        keys = dot(feats[...], factor[...], 1, 1) * inverse[...]
        for a in range(keys.shape[1]):
            wide[:, a * LANES : (a + 1) * LANES] = jnp.broadcast_to(keys[:, a : a + 1], (keys.shape[0], LANES))


def hold(x, after):
    args = [pltpu.with_memory_space_constraint(a, pltpu.VMEM) for a in [x, *after]]
    return pl.pallas_call(
        lambda *refs: None,
        out_shape=jax.ShapeDtypeStruct(x.shape, x.dtype),
        in_specs=[pl.BlockSpec(memory_space=pltpu.VMEM)] * len(args),
        out_specs=pl.BlockSpec(memory_space=pltpu.VMEM),
        input_output_aliases={0: 0},
        compiler_params=pltpu.CompilerParams(vmem_limit_bytes=1 << 20),
    )(*args)


def column_of(row):
    return jnp.broadcast_to(row, (LANES, LANES)).T


def lse_parts(scores, axis):
    top = jnp.max(scores, axis=axis, keepdims=True)
    return top, jnp.sum(jnp.exp(scores - top), axis=axis, keepdims=True)


def scores_kernel(ni, nt, *refs):
    images, texts = refs[:ni], refs[ni : ni + nt]
    raw, row_lse, col_top, col_total, all_images, all_texts = refs[ni + nt :]
    rows = images[0].shape[0]
    for a in range(ni):
        all_images[a * rows : (a + 1) * rows] = images[a][...]
    for t in range(nt):
        all_texts[t * rows : (t + 1) * rows] = texts[t][...]
    raw[...] = dot(all_images[...], all_texts[...], 1, 1)
    for a in range(ni):
        top, total = lse_parts(LOGIT_SCALE * raw[a * rows : (a + 1) * rows], 1)
        row_lse[a : a + 1] = jnp.broadcast_to(top + jnp.log(total), (rows, LANES)).T[:1]
    for t in range(nt):
        col_top[t : t + 1], col_total[t : t + 1] = lse_parts(LOGIT_SCALE * raw[:, t * rows : (t + 1) * rows], 0)


def last_scores_kernel(ni, nt, *refs):
    image, texts, (rows_lse, tops, totals) = refs[0], refs[1 : 1 + nt], refs[1 + nt : 4 + nt]
    raw, row_lse, col_lse, all_texts = refs[4 + nt :]
    rows = image.shape[0]
    for t in range(nt):
        all_texts[t * rows : (t + 1) * rows] = texts[t][...]
    raw[...] = dot(image[...], all_texts[...], 1, 1)
    top, total = lse_parts(LOGIT_SCALE * raw[...], 1)
    row_lse[: ni - 1] = rows_lse[...]
    row_lse[ni - 1 :] = jnp.broadcast_to(top + jnp.log(total), (rows, LANES)).T[:1]
    for t in range(nt):
        top, total = lse_parts(LOGIT_SCALE * raw[:, t * rows : (t + 1) * rows], 0)
        high = jnp.maximum(top, tops[t : t + 1])
        total = total * jnp.exp(top - high) + totals[t : t + 1] * jnp.exp(tops[t : t + 1] - high)
        col_lse[t : t + 1] = high + jnp.log(total)


def factors_kernel(ni, nt, *refs):
    images, texts, (b_img, b_txt) = refs[:ni], refs[ni : ni + nt], refs[ni + nt : ni + nt + 2]
    img_low, img_side_t, txt_low, txt_side_t, img_base, txt_base = refs[ni + nt + 2 :]
    rows = images[0].shape[0]
    for a in range(ni):
        here = slice(a * rows, (a + 1) * rows)
        low = dot(images[a][...], b_img[...])
        side = dot(images[a][...], b_txt[...])
        img_low[here] = low
        img_side_t[:, here] = side.T.astype(BF16)
        if a == 0:
            own_img_low, own_img_side = low, side.astype(BF16).astype(F32)
    for t in range(nt):
        here = slice(t * rows, (t + 1) * rows)
        low = dot(texts[t][...], b_img[...]).astype(BF16)
        side = dot(texts[t][...], b_txt[...])
        txt_low[here] = low
        txt_side_t[:, here] = side.T
        if t == 0:
            own_txt_low, own_txt_side = low.astype(F32), side
    diagonal = jnp.sum(
        images[0][...].astype(F32) * texts[0][...].astype(F32), axis=1, keepdims=True
    )
    img_base[...] = 2.0 * (diagonal * own_img_low - own_txt_low)
    txt_base[...] = 2.0 * (diagonal * own_txt_side - own_img_side)


def merge(parts, flips):
    slots = parts[0].shape[0]
    lined = [parts[0][...]]
    for k in range(1, len(parts)):
        lined.append(
            jnp.concatenate([parts[k][s ^ flips[k] :][:1] for s in range(slots)], axis=0)
        )
    top = functools.reduce(jnp.maximum, lined)
    return top + jnp.log(sum(jnp.exp(p - top) for p in lined))


def merge_kernel(flips, *refs):
    refs[-1][...] = merge(refs[:-1], flips)


def gather_lse(lse, bits, n):
    for j, bit in enumerate(bits[:-1]):
        (lse,) = call(functools.partial(merge_kernel, (0, 1 << j)), [(lse.shape, F32)], [lse, swap(lse, bit, n)])
    return [lse, swap(lse, bits[-1], n)], (0, 1 << len(bits) - 1)


def add_kernel(count, *refs):
    own, got, sent = refs[:count], refs[count:-1], refs[-1]
    rows = own[0].shape[0]
    for k in range(count):
        part = own[k][...]
        for arrived in got:
            at = (count + k) * rows
            part = part + arrived[at : at + rows].astype(F32)
        sent[k * rows : (k + 1) * rows] = part.astype(sent.dtype)


def halve(kept, sent, bits, n):
    rows = kept[0].shape[0]
    got = [swap(sent, bits[-1], n)]
    for bit in bits[-2::-1]:
        upper = kept[len(kept) // 2 :]
        (sent,) = call(
            functools.partial(add_kernel, len(upper)),
            [((len(upper) * rows, kept[0].shape[1]), BF16)],
            [*upper, *got],
        )
        kept = kept[: len(kept) // 2]
        got.append(swap(sent, bit, n))
    return [kept[0], *got], sent


def weights_kernel(ni, nt, row_flips, col_flips, *refs):
    row_parts, refs = refs[: len(row_flips)], refs[len(row_flips) :]
    col_parts, refs = refs[: len(col_flips)], refs[len(col_flips) :]
    raw, last_raw, img_low, txt_low = refs[:4]
    half = ni // 2
    *img_kept, img_sent, weights_bf, inners = refs[4:]
    rows = LANES
    row_lse = merge(row_parts, row_flips)
    col_lse = merge(col_parts, col_flips)
    inner_col = [jnp.zeros((1, rows), F32) for _ in range(nt)]
    for a in range(ni):
        row = column_of(row_lse[a : a + 1])
        inner_row = jnp.zeros((rows, rows), F32)
        for t in range(nt):
            cols = slice(t * rows, (t + 1) * rows)
            here = raw[a * rows : (a + 1) * rows, cols] if a < ni - 1 else last_raw[:, cols]
            scores = LOGIT_SCALE * here
            weights = jnp.exp(scores - row) + jnp.exp(scores - col_lse[t : t + 1])
            weights_bf[a * rows : (a + 1) * rows, t * rows : (t + 1) * rows] = weights.astype(BF16)
            weighted = weights * here
            inner_row = inner_row + weighted
            inner_col[t] = inner_col[t] + jnp.sum(weighted, axis=0, keepdims=True)
        inner = jnp.sum(inner_row, axis=1, keepdims=True)
        part = (
            dot(weights_bf[a * rows : (a + 1) * rows], txt_low[...])
            - inner * img_low[a * rows : (a + 1) * rows]
        )
        if a < half:
            img_kept[a][...] = part
        else:
            img_sent[(a - half) * rows : (a - half + 1) * rows] = part.astype(img_sent.dtype)
    for t in range(nt):
        inners[t : t + 1] = inner_col[t]


def columns_kernel(nt, weights_bf, inners, img_side_t, txt_side_t, *refs):
    rows, kept, sent = LANES, refs[:-1], refs[-1]
    for t in range(nt):
        here = slice(t * rows, (t + 1) * rows)
        part = dot(img_side_t[...], weights_bf[:, here]) - inners[t : t + 1] * txt_side_t[:, here]
        if t < nt // 2:
            kept[t][...] = part
        else:
            sent[(t - nt // 2) * rows : (t - nt // 2 + 1) * rows] = part.astype(sent.dtype)


def sketch_kernel(count, turned, *refs):
    parts, (base, keys, out, made, sems) = refs[:count], refs[count:]
    rows = base.shape[0]
    grad = sum((part[:rows].astype(F32) for part in parts[1:]), parts[0][...])
    grad = (grad.T if turned else grad) + base[...]
    copies, step = [], rows // 2
    for k in range(2):
        here = slice(k * step, (k + 1) * step)
        for a in range(0, made.shape[1], LANES):
            made[here, a : a + LANES] = (keys[here, a : a + LANES] * grad[here]).astype(BF16)
        copies.append(pltpu.make_async_copy(made.at[here], out.at[here], sems.at[k]))
        copies[-1].start()
    for copy in copies:
        copy.wait()


def sketch(parts, base, keys, turned):
    args = [pltpu.with_memory_space_constraint(a, pltpu.VMEM) for a in [*parts, base, keys]]
    return pl.pallas_call(
        functools.partial(sketch_kernel, len(parts), turned),
        out_shape=jax.ShapeDtypeStruct(keys.shape, BF16),
        in_specs=[pl.BlockSpec(memory_space=pltpu.VMEM)] * len(args),
        out_specs=pl.BlockSpec(memory_space=pltpu.HBM),
        scratch_shapes=[pltpu.VMEM(keys.shape, BF16), pltpu.SemaphoreType.DMA((2,))],
        compiler_params=pltpu.CompilerParams(vmem_limit_bytes=16 << 20),
        cost_estimate=pl.CostEstimate(flops=keys.size, bytes_accessed=6 * keys.size, transcendentals=0),
    )(*args)


def body(n, img_feats, txt_feats, w_img, w_txt, a_img, b_img, a_txt, b_txt):
    rows, wide = img_feats.shape[0], w_img.shape[1]
    low = b_img.shape[1]
    assert rows == LANES and low == LANES
    img_bits, txt_bits = split_bits(n)
    img_span, txt_span = span(img_bits), span(txt_bits)
    ni, nt = len(img_span), len(txt_span)
    (img_emb,), img_inv = stream_embed([img_feats], w_img, False)
    far = gather(txt_feats, txt_bits[:-1], n)
    near = swap(txt_feats, txt_bits[-1], n)
    (txt_emb,), txt_inv, w_txt_v = stream_embed([txt_feats], w_txt, True)
    far = [txt_emb] + [embed([x], w_txt_v)[0] for x in far[1:]]
    texts = far + embed([near], w_txt_v) + [swap(x, txt_bits[-1], n) for x in far[1:]]
    img_keys, txt_keys = call(
        keys_kernel,
        [((rows, a_img.shape[1] * LANES), F32), ((rows, a_txt.shape[1] * LANES), F32)],
        [img_feats, txt_feats, a_img.T, a_txt.T, img_inv, txt_inv],
    )
    images = gather(img_emb, img_bits, n, lambda x: hold(x, [texts[nt // 2], img_keys]))
    raw, rows_lse, tops, totals = call(
        functools.partial(scores_kernel, ni - 1, nt),
        [(((ni - 1) * rows, nt * rows), F32), ((ni - 1, rows), F32), ((nt, rows), F32), ((nt, rows), F32)],
        images[:-1] + texts,
        scratch=[pltpu.VMEM(((ni - 1) * rows, wide), BF16), pltpu.VMEM((nt * rows, wide), BF16)],
        flops=2 * (ni - 1) * nt * rows * rows * wide,
    )
    last_raw, row_lse, col_lse = call(
        functools.partial(last_scores_kernel, ni, nt),
        [((rows, nt * rows), F32), ((ni, rows), F32), ((nt, rows), F32)],
        images[-1:] + texts + [rows_lse, tops, totals],
        scratch=[pltpu.VMEM((nt * rows, wide), BF16)],
        flops=2 * nt * rows * rows * wide,
    )
    row_parts = gather(row_lse, img_bits, n)
    col_parts, col_flips = gather_lse(col_lse, txt_bits, n)
    img_low, img_side_t, txt_low, txt_side_t, img_base, txt_base = call(
        functools.partial(factors_kernel, ni, nt),
        [
            ((ni * rows, low), F32),
            ((low, ni * rows), BF16),
            ((nt * rows, low), BF16),
            ((low, nt * rows), F32),
            ((rows, low), F32),
            ((rows, low), F32),
        ],
        images + texts + [b_img, b_txt],
        flops=4 * (ni + nt) * rows * wide * low,
    )
    half = ni // 2
    *img_kept, img_sent, weights_bf, inners = call(
        functools.partial(weights_kernel, ni, nt, tuple(range(ni)), col_flips),
        [((rows, low), F32)] * half
        + [((half * rows, low), BF16), ((ni * rows, nt * rows), BF16), ((nt, rows), F32)],
        row_parts + col_parts + [raw, last_raw, img_low, txt_low],
        flops=2 * ni * nt * rows * rows * low,
    )
    *txt_kept, txt_sent = call(
        functools.partial(columns_kernel, nt),
        [((rows, low), F32)] * (nt // 2) + [((nt // 2 * rows, low), BF16)],
        [weights_bf, inners, img_side_t, txt_side_t],
        flops=2 * ni * nt * rows * rows * low,
    )
    img_parts, _ = halve(img_kept, img_sent, img_bits, n)
    txt_parts, _ = halve(txt_kept, txt_sent, txt_bits, n)
    return (
        sketch(img_parts, img_base, img_keys, False),
        sketch(txt_parts, txt_base, txt_keys, True),
    )


def solution(mesh):
    n = mesh.shape["dp"]
    rows = P(("ckpt", "dp"), None)
    part = P("ckpt", None)
    return jax.shard_map(
        lambda *args: body(n, *args),
        mesh=mesh,
        in_specs=(rows, rows, part, part, P(), P(), P(), P()),
        out_specs=(rows, rows),
        check_vma=False,
    )
```

```python
import functools
import jax
import jax.numpy as jnp
from jax import lax
from jax.experimental import pallas as pl
from jax.experimental.pallas import tpu as pltpu
from jax.sharding import PartitionSpec as P

LOGIT_SCALE = 100.0
EPSILON = 1e-06
F32 = jnp.float32
BF16 = jnp.bfloat16
LANES = 128
PIECES = 4


def dot(left, right, left_dim=1, right_dim=0):
    return lax.dot_general(
        left, right, (((left_dim,), (right_dim,)), ((), ())), preferred_element_type=F32
    )


def skip(kernel, first, count, *refs):
    kernel(*refs[:first], *refs[first + count :])


def call(kernel, outs, args, after=(), free=(), scratch=(), flops=0, limit=16):
    args = [a if k in free else pltpu.with_memory_space_constraint(a, pltpu.VMEM) for k, a in enumerate(args)]
    size = sum(a.size * a.dtype.itemsize for a in args)
    specs = [pl.BlockSpec(memory_space=pltpu.VMEM)] * len(args)
    if after:
        kernel = functools.partial(skip, kernel, len(args), len(after))
        args, specs = args + list(after), specs + [pl.BlockSpec(memory_space=pl.ANY)] * len(after)
    return pl.pallas_call(
        kernel,
        out_shape=[jax.ShapeDtypeStruct(s, d) for s, d in outs],
        in_specs=specs,
        out_specs=[pl.BlockSpec(memory_space=pltpu.VMEM)] * len(outs),
        scratch_shapes=list(scratch),
        compiler_params=pltpu.CompilerParams(vmem_limit_bytes=limit << 20),
        cost_estimate=pl.CostEstimate(flops=flops, bytes_accessed=size, transcendentals=0),
    )(*args)


def span(bits):
    offsets = [0]
    for bit in bits:
        offsets = offsets + [o ^ bit for o in offsets]
    return offsets


def split_bits(n):
    bits = [1 << b for b in range(n.bit_length() - 1)]
    assert 1 << len(bits) == n
    half = len(bits) // 2
    return bits[:half:-1] + bits[:1], bits[half:0:-1]


def swap(x, offset, n):
    return lax.ppermute(x, "dp", [(i, i ^ offset) for i in range(n)])


def gather(block, bits, n, ready=None):
    blocks = [block]
    for bit in bits:
        new = [swap(b, bit, n) for b in blocks]
        blocks = blocks + (new if ready is None or bit == bits[-1] else [ready(b) for b in new])
    return blocks


def normalised(raw):
    inverse = lax.rsqrt(jnp.sum(raw * raw, axis=1, keepdims=True) + EPSILON)
    return (raw * inverse).astype(BF16), inverse


def embed_kernel(blocks, *refs):
    feats, weight, embs = refs[:blocks], refs[blocks], refs[blocks + 1 :]
    for b in range(blocks):
        embs[b][...] = normalised(dot(feats[b][...], weight[...]))[0]


def embed(feats, weight):
    rows, blocks = feats[0].shape[0], len(feats)
    return list(
        call(
            functools.partial(embed_kernel, blocks),
            [((rows, weight.shape[1]), BF16)] * blocks,
            [*feats, weight],
            flops=2 * blocks * rows * weight.size,
        )
    )


def stream_kernel(blocks, cuts, *refs):
    feats, weight, embs = refs[:blocks], refs[blocks], refs[blocks + 1 : 2 * blocks + 1]
    inverse, weight_v, own_v, sems = refs[2 * blocks + 1 :]
    own = pltpu.make_async_copy(feats[0], own_v, sems.at[0])
    pieces = [slice(lo, hi) for lo, hi in zip(cuts, cuts[1:])]
    copies = [
        pltpu.make_async_copy(weight.at[p], weight_v.at[p], sems.at[1 + k]) for k, p in enumerate(pieces)
    ]
    for copy in [own, *copies]:
        copy.start()
    own.wait()
    raws = [0.0] * blocks
    for p, copy in zip(pieces, copies):
        copy.wait()
        for b in range(blocks):
            left = own_v[:, p] if b == 0 else feats[b][:, p]
            raws[b] = raws[b] + dot(left, weight_v[p])
    embs[0][...], inverse[...] = normalised(raws[0])
    for b in range(1, blocks):
        embs[b][...] = normalised(raws[b])[0]


def stream_embed(feats, weight, keep):
    (rows, depth), blocks = feats[0].shape, len(feats)
    cuts = [depth // LANES * k // PIECES * LANES for k in range(PIECES)] + [depth]
    far = [pltpu.with_memory_space_constraint(a, pltpu.HBM) for a in (feats[0], weight)]
    near = [pltpu.with_memory_space_constraint(a, pltpu.VMEM) for a in feats[1:]]
    hbm, vmem = pl.BlockSpec(memory_space=pltpu.HBM), pl.BlockSpec(memory_space=pltpu.VMEM)
    outs = [((rows, weight.shape[1]), BF16)] * blocks + [((rows, 1), F32)] + [(weight.shape, BF16)] * keep
    out = pl.pallas_call(
        functools.partial(stream_kernel, blocks, cuts),
        out_shape=[jax.ShapeDtypeStruct(*o) for o in outs],
        in_specs=[hbm] + [vmem] * (blocks - 1) + [hbm],
        out_specs=[vmem] * len(outs),
        scratch_shapes=[pltpu.VMEM(weight.shape, BF16)] * (not keep)
        + [pltpu.VMEM((rows, depth), BF16), pltpu.SemaphoreType.DMA((PIECES + 1,))],
        compiler_params=pltpu.CompilerParams(vmem_limit_bytes=16 << 20),
        cost_estimate=pl.CostEstimate(
            flops=2 * blocks * rows * weight.size, bytes_accessed=2 * weight.size, transcendentals=0
        ),
    )(far[0], *near, far[1])
    return list(out[:blocks]), *out[blocks:]


def keys_kernel(*refs):
    for feats, factor, inverse, wide in zip(refs[:2], refs[2:4], refs[4:6], refs[6:8]):
        keys = dot(feats[...], factor[...], 1, 1) * inverse[...]
        for a in range(keys.shape[1]):
            wide[:, a * LANES : (a + 1) * LANES] = jnp.broadcast_to(keys[:, a : a + 1], (keys.shape[0], LANES))


def hold(x, after):
    args = [pltpu.with_memory_space_constraint(a, pltpu.VMEM) for a in [x, *after]]
    return pl.pallas_call(
        lambda *refs: None,
        out_shape=jax.ShapeDtypeStruct(x.shape, x.dtype),
        in_specs=[pl.BlockSpec(memory_space=pltpu.VMEM)] * len(args),
        out_specs=pl.BlockSpec(memory_space=pltpu.VMEM),
        input_output_aliases={0: 0},
        compiler_params=pltpu.CompilerParams(vmem_limit_bytes=1 << 20),
    )(*args)


def column_of(row):
    return jnp.broadcast_to(row, (LANES, LANES)).T


def lse_parts(scores, axis):
    top = jnp.max(scores, axis=axis, keepdims=True)
    return top, jnp.sum(jnp.exp(scores - top), axis=axis, keepdims=True)


def scores_kernel(ni, nt, *refs):
    images, texts = refs[:ni], refs[ni : ni + nt]
    raw, row_lse, col_top, col_total, all_images, all_texts = refs[ni + nt :]
    rows = images[0].shape[0]
    for a in range(ni):
        all_images[a * rows : (a + 1) * rows] = images[a][...]
    for t in range(nt):
        all_texts[t * rows : (t + 1) * rows] = texts[t][...]
    raw[...] = dot(all_images[...], all_texts[...], 1, 1)
    for a in range(ni):
        top, total = lse_parts(LOGIT_SCALE * raw[a * rows : (a + 1) * rows], 1)
        row_lse[a : a + 1] = jnp.broadcast_to(top + jnp.log(total), (rows, LANES)).T[:1]
    for t in range(nt):
        col_top[t : t + 1], col_total[t : t + 1] = lse_parts(LOGIT_SCALE * raw[:, t * rows : (t + 1) * rows], 0)


def last_scores_kernel(ni, nt, *refs):
    image, texts, (rows_lse, tops, totals) = refs[0], refs[1 : 1 + nt], refs[1 + nt : 4 + nt]
    raw, row_lse, col_lse, all_texts = refs[4 + nt :]
    rows = image.shape[0]
    for t in range(nt):
        all_texts[t * rows : (t + 1) * rows] = texts[t][...]
    raw[...] = dot(image[...], all_texts[...], 1, 1)
    top, total = lse_parts(LOGIT_SCALE * raw[...], 1)
    row_lse[: ni - 1] = rows_lse[...]
    row_lse[ni - 1 :] = jnp.broadcast_to(top + jnp.log(total), (rows, LANES)).T[:1]
    for t in range(nt):
        top, total = lse_parts(LOGIT_SCALE * raw[:, t * rows : (t + 1) * rows], 0)
        high = jnp.maximum(top, tops[t : t + 1])
        total = total * jnp.exp(top - high) + totals[t : t + 1] * jnp.exp(tops[t : t + 1] - high)
        col_lse[t : t + 1] = high + jnp.log(total)


def factors_kernel(ni, nt, *refs):
    images, texts, (b_img, b_txt) = refs[:ni], refs[ni : ni + nt], refs[ni + nt : ni + nt + 2]
    img_low, img_side_t, txt_low, txt_side_t, img_base, txt_base = refs[ni + nt + 2 :]
    rows = images[0].shape[0]
    for a in range(ni):
        here = slice(a * rows, (a + 1) * rows)
        low = dot(images[a][...], b_img[...])
        side = dot(images[a][...], b_txt[...])
        img_low[here] = low
        img_side_t[:, here] = side.T.astype(BF16)
        if a == 0:
            own_img_low, own_img_side = low, side.astype(BF16).astype(F32)
    for t in range(nt):
        here = slice(t * rows, (t + 1) * rows)
        low = dot(texts[t][...], b_img[...]).astype(BF16)
        side = dot(texts[t][...], b_txt[...])
        txt_low[here] = low
        txt_side_t[:, here] = side.T
        if t == 0:
            own_txt_low, own_txt_side = low.astype(F32), side
    diagonal = jnp.sum(
        images[0][...].astype(F32) * texts[0][...].astype(F32), axis=1, keepdims=True
    )
    img_base[...] = 2.0 * (diagonal * own_img_low - own_txt_low)
    txt_base[...] = 2.0 * (diagonal * own_txt_side - own_img_side)


def merge(parts, flips):
    slots = parts[0].shape[0]
    lined = [parts[0][...]]
    for k in range(1, len(parts)):
        lined.append(
            jnp.concatenate([parts[k][s ^ flips[k] :][:1] for s in range(slots)], axis=0)
        )
    top = functools.reduce(jnp.maximum, lined)
    return top + jnp.log(sum(jnp.exp(p - top) for p in lined))


def merge_kernel(flips, *refs):
    refs[-1][...] = merge(refs[:-1], flips)


def gather_lse(lse, bits, n):
    for j, bit in enumerate(bits[:-1]):
        (lse,) = call(functools.partial(merge_kernel, (0, 1 << j)), [(lse.shape, F32)], [lse, swap(lse, bit, n)])
    return [lse, swap(lse, bits[-1], n)], (0, 1 << len(bits) - 1)


def add_kernel(count, *refs):
    own, got, sent = refs[:count], refs[count:-1], refs[-1]
    rows = own[0].shape[0]
    for k in range(count):
        part = own[k][...]
        for arrived in got:
            at = (count + k) * rows
            part = part + arrived[at : at + rows].astype(F32)
        sent[k * rows : (k + 1) * rows] = part.astype(sent.dtype)


def halve(kept, sent, bits, n):
    rows = kept[0].shape[0]
    got = [swap(sent, bits[-1], n)]
    for bit in bits[-2::-1]:
        upper = kept[len(kept) // 2 :]
        (sent,) = call(
            functools.partial(add_kernel, len(upper)),
            [((len(upper) * rows, kept[0].shape[1]), BF16)],
            [*upper, *got],
        )
        kept = kept[: len(kept) // 2]
        got.append(swap(sent, bit, n))
    return [kept[0], *got], sent


def weights_kernel(ni, nt, row_flips, col_flips, *refs):
    row_parts, refs = refs[: len(row_flips)], refs[len(row_flips) :]
    col_parts, refs = refs[: len(col_flips)], refs[len(col_flips) :]
    raw, last_raw, img_low, txt_low = refs[:4]
    half = ni // 2
    *img_kept, img_sent, weights_bf, inners = refs[4:]
    rows = LANES
    row_lse = merge(row_parts, row_flips)
    col_lse = merge(col_parts, col_flips)
    inner_col = [jnp.zeros((1, rows), F32) for _ in range(nt)]
    for a in range(ni):
        row = column_of(row_lse[a : a + 1])
        inner_row = jnp.zeros((rows, rows), F32)
        for t in range(nt):
            cols = slice(t * rows, (t + 1) * rows)
            here = raw[a * rows : (a + 1) * rows, cols] if a < ni - 1 else last_raw[:, cols]
            scores = LOGIT_SCALE * here
            weights = jnp.exp(scores - row) + jnp.exp(scores - col_lse[t : t + 1])
            weights_bf[a * rows : (a + 1) * rows, t * rows : (t + 1) * rows] = weights.astype(BF16)
            weighted = weights * here
            inner_row = inner_row + weighted
            inner_col[t] = inner_col[t] + jnp.sum(weighted, axis=0, keepdims=True)
        inner = jnp.sum(inner_row, axis=1, keepdims=True)
        part = (
            dot(weights_bf[a * rows : (a + 1) * rows], txt_low[...])
            - inner * img_low[a * rows : (a + 1) * rows]
        )
        if a < half:
            img_kept[a][...] = part
        else:
            img_sent[(a - half) * rows : (a - half + 1) * rows] = part.astype(img_sent.dtype)
    for t in range(nt):
        inners[t : t + 1] = inner_col[t]


def columns_kernel(nt, weights_bf, inners, img_side_t, txt_side_t, *refs):
    rows, kept, sent = LANES, refs[:-1], refs[-1]
    for t in range(nt):
        here = slice(t * rows, (t + 1) * rows)
        part = dot(img_side_t[...], weights_bf[:, here]) - inners[t : t + 1] * txt_side_t[:, here]
        if t < nt // 2:
            kept[t][...] = part
        else:
            sent[(t - nt // 2) * rows : (t - nt // 2 + 1) * rows] = part.astype(sent.dtype)


def sketch_kernel(count, turned, *refs):
    parts, (base, keys, out, made, sems) = refs[:count], refs[count:]
    rows = base.shape[0]
    grad = sum((part[:rows].astype(F32) for part in parts[1:]), parts[0][...])
    grad = (grad.T if turned else grad) + base[...]
    copies, step = [], rows // 2
    for k in range(2):
        here = slice(k * step, (k + 1) * step)
        for a in range(0, made.shape[1], LANES):
            made[here, a : a + LANES] = (keys[here, a : a + LANES] * grad[here]).astype(BF16)
        copies.append(pltpu.make_async_copy(made.at[here], out.at[here], sems.at[k]))
        copies[-1].start()
    for copy in copies:
        copy.wait()


def sketch(parts, base, keys, turned):
    args = [pltpu.with_memory_space_constraint(a, pltpu.VMEM) for a in [*parts, base, keys]]
    return pl.pallas_call(
        functools.partial(sketch_kernel, len(parts), turned),
        out_shape=jax.ShapeDtypeStruct(keys.shape, BF16),
        in_specs=[pl.BlockSpec(memory_space=pltpu.VMEM)] * len(args),
        out_specs=pl.BlockSpec(memory_space=pltpu.HBM),
        scratch_shapes=[pltpu.VMEM(keys.shape, BF16), pltpu.SemaphoreType.DMA((2,))],
        compiler_params=pltpu.CompilerParams(vmem_limit_bytes=16 << 20),
        cost_estimate=pl.CostEstimate(flops=keys.size, bytes_accessed=6 * keys.size, transcendentals=0),
    )(*args)


def body(n, img_feats, txt_feats, w_img, w_txt, a_img, b_img, a_txt, b_txt):
    rows, wide = img_feats.shape[0], w_img.shape[1]
    low = b_img.shape[1]
    assert rows == LANES and low == LANES
    img_bits, txt_bits = split_bits(n)
    img_span, txt_span = span(img_bits), span(txt_bits)
    ni, nt = len(img_span), len(txt_span)
    (img_emb,), img_inv = stream_embed([img_feats], w_img, False)
    far = gather(txt_feats, txt_bits[:-1], n)
    near = swap(txt_feats, txt_bits[-1], n)
    (txt_emb,), txt_inv, w_txt_v = stream_embed([txt_feats], w_txt, True)
    far = [txt_emb] + [embed([x], w_txt_v)[0] for x in far[1:]]
    onward = [swap(x, txt_bits[-1], n) for x in far[1:]]
    texts = far + embed([near], w_txt_v) + onward
    img_keys, txt_keys = call(
        keys_kernel,
        [((rows, a_img.shape[1] * LANES), F32), ((rows, a_txt.shape[1] * LANES), F32)],
        [img_feats, txt_feats, a_img.T, a_txt.T, img_inv, txt_inv],
    )
    images = gather(img_emb, img_bits, n, lambda x: hold(x, [texts[0], img_keys]))
    raw, rows_lse, tops, totals = call(
        functools.partial(scores_kernel, ni - 1, nt),
        [(((ni - 1) * rows, nt * rows), F32), ((ni - 1, rows), F32), ((nt, rows), F32), ((nt, rows), F32)],
        images[:-1] + texts,
        scratch=[pltpu.VMEM(((ni - 1) * rows, wide), BF16), pltpu.VMEM((nt * rows, wide), BF16)],
        flops=2 * (ni - 1) * nt * rows * rows * wide,
    )
    last_raw, row_lse, col_lse = call(
        functools.partial(last_scores_kernel, ni, nt),
        [((rows, nt * rows), F32), ((ni, rows), F32), ((nt, rows), F32)],
        images[-1:] + texts + [rows_lse, tops, totals],
        scratch=[pltpu.VMEM((nt * rows, wide), BF16)],
        flops=2 * nt * rows * rows * wide,
    )
    row_parts = gather(row_lse, img_bits, n)
    col_parts, col_flips = gather_lse(col_lse, txt_bits, n)
    img_low, img_side_t, txt_low, txt_side_t, img_base, txt_base = call(
        functools.partial(factors_kernel, ni, nt),
        [
            ((ni * rows, low), F32),
            ((low, ni * rows), BF16),
            ((nt * rows, low), BF16),
            ((low, nt * rows), F32),
            ((rows, low), F32),
            ((rows, low), F32),
        ],
        images + texts + [b_img, b_txt],
        flops=4 * (ni + nt) * rows * wide * low,
    )
    half = ni // 2
    *img_kept, img_sent, weights_bf, inners = call(
        functools.partial(weights_kernel, ni, nt, tuple(range(ni)), col_flips),
        [((rows, low), F32)] * half
        + [((half * rows, low), BF16), ((ni * rows, nt * rows), BF16), ((nt, rows), F32)],
        row_parts + col_parts + [raw, last_raw, img_low, txt_low],
        flops=2 * ni * nt * rows * rows * low,
    )
    *txt_kept, txt_sent = call(
        functools.partial(columns_kernel, nt),
        [((rows, low), F32)] * (nt // 2) + [((nt // 2 * rows, low), BF16)],
        [weights_bf, inners, img_side_t, txt_side_t],
        flops=2 * ni * nt * rows * rows * low,
    )
    img_parts, _ = halve(img_kept, img_sent, img_bits, n)
    txt_parts, _ = halve(txt_kept, txt_sent, txt_bits, n)
    return (
        sketch(img_parts, img_base, img_keys, False),
        sketch(txt_parts, txt_base, txt_keys, True),
    )


def solution(mesh):
    n = mesh.shape["dp"]
    rows = P(("ckpt", "dp"), None)
    part = P("ckpt", None)
    return jax.shard_map(
        lambda *args: body(n, *args),
        mesh=mesh,
        in_specs=(rows, rows, part, part, P(), P(), P(), P()),
        out_specs=(rows, rows),
        check_vma=False,
    )
```

```python
import functools
import jax
import jax.numpy as jnp
from jax import lax
from jax.experimental import pallas as pl
from jax.experimental.pallas import tpu as pltpu
from jax.sharding import PartitionSpec as P

LOGIT_SCALE = 100.0
EPSILON = 1e-06
F32 = jnp.float32
BF16 = jnp.bfloat16
LANES = 128
PIECES = 4


def dot(left, right, left_dim=1, right_dim=0):
    return lax.dot_general(
        left, right, (((left_dim,), (right_dim,)), ((), ())), preferred_element_type=F32
    )


def skip(kernel, first, count, *refs):
    kernel(*refs[:first], *refs[first + count :])


def call(kernel, outs, args, after=(), free=(), scratch=(), flops=0, limit=16):
    args = [a if k in free else pltpu.with_memory_space_constraint(a, pltpu.VMEM) for k, a in enumerate(args)]
    size = sum(a.size * a.dtype.itemsize for a in args)
    specs = [pl.BlockSpec(memory_space=pltpu.VMEM)] * len(args)
    if after:
        kernel = functools.partial(skip, kernel, len(args), len(after))
        args += [pltpu.with_memory_space_constraint(a, pltpu.VMEM) for a in after]
        specs += [pl.BlockSpec(memory_space=pltpu.VMEM)] * len(after)
    return pl.pallas_call(
        kernel,
        out_shape=[jax.ShapeDtypeStruct(s, d) for s, d in outs],
        in_specs=specs,
        out_specs=[pl.BlockSpec(memory_space=pltpu.VMEM)] * len(outs),
        scratch_shapes=list(scratch),
        compiler_params=pltpu.CompilerParams(vmem_limit_bytes=limit << 20),
        cost_estimate=pl.CostEstimate(flops=flops, bytes_accessed=size, transcendentals=0),
    )(*args)


def span(bits):
    offsets = [0]
    for bit in bits:
        offsets = offsets + [o ^ bit for o in offsets]
    return offsets


def split_bits(n):
    bits = [1 << b for b in range(n.bit_length() - 1)]
    assert 1 << len(bits) == n
    half = len(bits) // 2
    return bits[:half:-1] + bits[:1], bits[half:0:-1]


def swap(x, offset, n):
    return lax.ppermute(x, "dp", [(i, i ^ offset) for i in range(n)])


def gather(block, bits, n, ready=None):
    blocks = [block]
    for bit in bits:
        new = [swap(b, bit, n) for b in blocks]
        blocks = blocks + (new if ready is None or bit == bits[-1] else [ready(b) for b in new])
    return blocks


def normalised(raw):
    inverse = lax.rsqrt(jnp.sum(raw * raw, axis=1, keepdims=True) + EPSILON)
    return (raw * inverse).astype(BF16), inverse


def embed_kernel(blocks, *refs):
    feats, weight, embs = refs[:blocks], refs[blocks], refs[blocks + 1 :]
    for b in range(blocks):
        embs[b][...] = normalised(dot(feats[b][...], weight[...]))[0]


def embed(feats, weight):
    rows, blocks = feats[0].shape[0], len(feats)
    return list(
        call(
            functools.partial(embed_kernel, blocks),
            [((rows, weight.shape[1]), BF16)] * blocks,
            [*feats, weight],
            flops=2 * blocks * rows * weight.size,
        )
    )


def stream_kernel(blocks, cuts, *refs):
    feats, weight, embs = refs[:blocks], refs[blocks], refs[blocks + 1 : 2 * blocks + 1]
    inverse, weight_v, own_v, sems = refs[2 * blocks + 1 :]
    own = pltpu.make_async_copy(feats[0], own_v, sems.at[0])
    pieces = [slice(lo, hi) for lo, hi in zip(cuts, cuts[1:])]
    copies = [
        pltpu.make_async_copy(weight.at[p], weight_v.at[p], sems.at[1 + k]) for k, p in enumerate(pieces)
    ]
    for copy in [own, *copies]:
        copy.start()
    own.wait()
    raws = [0.0] * blocks
    for p, copy in zip(pieces, copies):
        copy.wait()
        for b in range(blocks):
            left = own_v[:, p] if b == 0 else feats[b][:, p]
            raws[b] = raws[b] + dot(left, weight_v[p])
    embs[0][...], inverse[...] = normalised(raws[0])
    for b in range(1, blocks):
        embs[b][...] = normalised(raws[b])[0]


def stream_embed(feats, weight, keep):
    (rows, depth), blocks = feats[0].shape, len(feats)
    cuts = [depth // LANES * k // PIECES * LANES for k in range(PIECES)] + [depth]
    far = [pltpu.with_memory_space_constraint(a, pltpu.HBM) for a in (feats[0], weight)]
    near = [pltpu.with_memory_space_constraint(a, pltpu.VMEM) for a in feats[1:]]
    hbm, vmem = pl.BlockSpec(memory_space=pltpu.HBM), pl.BlockSpec(memory_space=pltpu.VMEM)
    outs = [((rows, weight.shape[1]), BF16)] * blocks + [((rows, 1), F32)] + [(weight.shape, BF16)] * keep
    out = pl.pallas_call(
        functools.partial(stream_kernel, blocks, cuts),
        out_shape=[jax.ShapeDtypeStruct(*o) for o in outs],
        in_specs=[hbm] + [vmem] * (blocks - 1) + [hbm],
        out_specs=[vmem] * len(outs),
        scratch_shapes=[pltpu.VMEM(weight.shape, BF16)] * (not keep)
        + [pltpu.VMEM((rows, depth), BF16), pltpu.SemaphoreType.DMA((PIECES + 1,))],
        compiler_params=pltpu.CompilerParams(vmem_limit_bytes=16 << 20),
        cost_estimate=pl.CostEstimate(
            flops=2 * blocks * rows * weight.size, bytes_accessed=2 * weight.size, transcendentals=0
        ),
    )(far[0], *near, far[1])
    return list(out[:blocks]), *out[blocks:]


def keys_kernel(*refs):
    for feats, factor, inverse, wide in zip(refs[:2], refs[2:4], refs[4:6], refs[6:8]):
        keys = dot(feats[...], factor[...], 1, 1) * inverse[...]
        for a in range(keys.shape[1]):
            wide[:, a * LANES : (a + 1) * LANES] = jnp.broadcast_to(keys[:, a : a + 1], (keys.shape[0], LANES))


def hold(x, after):
    args = [pltpu.with_memory_space_constraint(a, pltpu.VMEM) for a in [x, *after]]
    return pl.pallas_call(
        lambda *refs: None,
        out_shape=jax.ShapeDtypeStruct(x.shape, x.dtype),
        in_specs=[pl.BlockSpec(memory_space=pltpu.VMEM)] * len(args),
        out_specs=pl.BlockSpec(memory_space=pltpu.VMEM),
        input_output_aliases={0: 0},
        compiler_params=pltpu.CompilerParams(vmem_limit_bytes=1 << 20),
    )(*args)


def column_of(row):
    return jnp.broadcast_to(row, (LANES, LANES)).T


def lse_parts(scores, axis):
    top = jnp.max(scores, axis=axis, keepdims=True)
    return top, jnp.sum(jnp.exp(scores - top), axis=axis, keepdims=True)


def lay(blocks, whole):
    rows = blocks[0].shape[0]
    for k, block in enumerate(blocks):
        whole[k * rows : (k + 1) * rows] = block[...]


def scores_kernel(ni, nt, *refs):
    images, texts, refs = refs[:ni], refs[ni : ni + nt], refs[ni + nt :]
    raw, row_top, row_total, col_top, col_total, all_images, all_texts = refs
    rows = images[0].shape[0]
    lay(images, all_images)
    lay(texts, all_texts)
    raw[...] = dot(all_images[...], all_texts[...], 1, 1)
    row_top[...], row_total[...] = lse_parts(LOGIT_SCALE * raw[...], 1)
    for t in range(nt):
        col_top[t : t + 1], col_total[t : t + 1] = lse_parts(LOGIT_SCALE * raw[:, t * rows : (t + 1) * rows], 0)


def joined(top, total, other_top, other_total):
    high = jnp.maximum(top, other_top)
    return high + jnp.log(total * jnp.exp(top - high) + other_total * jnp.exp(other_top - high))


def last_scores_kernel(ni, nt, *refs):
    images, texts, refs = refs[:ni], refs[ni : ni + nt], refs[ni + nt :]
    row_top, row_total, col_top, col_total, last_col, last_row, row_lse, col_lse, all_images, all_texts = refs
    rows = images[0].shape[0]
    lay(images[:-1], all_images)
    lay(texts, all_texts)
    last_col[...] = dot(all_images[...], texts[-1][...], 1, 1)
    last_row[...] = dot(images[-1][...], all_texts[...], 1, 1)
    col_scores, row_scores = LOGIT_SCALE * last_col[...], LOGIT_SCALE * last_row[...]
    lse = joined(row_top[...], row_total[...], *lse_parts(col_scores, 1))
    top, total = lse_parts(row_scores, 1)
    lses = [lse[a * rows : (a + 1) * rows] for a in range(ni - 1)] + [top + jnp.log(total)]
    for a in range(ni):
        row_lse[a : a + 1] = jnp.broadcast_to(lses[a], (rows, LANES)).T[:1]
    for t in range(nt):
        top, total = lse_parts(row_scores[:, t * rows : (t + 1) * rows], 0)
        if t < nt - 1:
            others = col_top[t : t + 1], col_total[t : t + 1]
        else:
            others = lse_parts(col_scores, 0)
        col_lse[t : t + 1] = joined(top, total, *others)


def factors_kernel(ni, nt, *refs):
    images, texts, (b_img, b_txt) = refs[:ni], refs[ni : ni + nt], refs[ni + nt : ni + nt + 2]
    img_low, img_side_t, txt_low, txt_side_t, img_base, txt_base = refs[ni + nt + 2 :]
    rows = images[0].shape[0]
    for a in range(ni):
        here = slice(a * rows, (a + 1) * rows)
        low = dot(images[a][...], b_img[...])
        side = dot(images[a][...], b_txt[...])
        img_low[here] = low
        img_side_t[:, here] = side.T.astype(BF16)
        if a == 0:
            own_img_low, own_img_side = low, side.astype(BF16).astype(F32)
    for t in range(nt):
        here = slice(t * rows, (t + 1) * rows)
        low = dot(texts[t][...], b_img[...]).astype(BF16)
        side = dot(texts[t][...], b_txt[...])
        txt_low[here] = low
        txt_side_t[:, here] = side.T
        if t == 0:
            own_txt_low, own_txt_side = low.astype(F32), side
    diagonal = jnp.sum(
        images[0][...].astype(F32) * texts[0][...].astype(F32), axis=1, keepdims=True
    )
    img_base[...] = 2.0 * (diagonal * own_img_low - own_txt_low)
    txt_base[...] = 2.0 * (diagonal * own_txt_side - own_img_side)


def merge(parts, flips):
    slots = parts[0].shape[0]
    lined = [parts[0][...]]
    for k in range(1, len(parts)):
        lined.append(
            jnp.concatenate([parts[k][s ^ flips[k] :][:1] for s in range(slots)], axis=0)
        )
    top = functools.reduce(jnp.maximum, lined)
    return top + jnp.log(sum(jnp.exp(p - top) for p in lined))


def merge_kernel(flips, *refs):
    refs[-1][...] = merge(refs[:-1], flips)


def gather_lse(lse, bits, n):
    for j, bit in enumerate(bits[:-1]):
        (lse,) = call(functools.partial(merge_kernel, (0, 1 << j)), [(lse.shape, F32)], [lse, swap(lse, bit, n)])
    return [lse, swap(lse, bits[-1], n)], (0, 1 << len(bits) - 1)


def add_kernel(count, *refs):
    own, got, sent = refs[:count], refs[count:-1], refs[-1]
    rows = own[0].shape[0]
    for k in range(count):
        part = own[k][...]
        for arrived in got:
            at = (count + k) * rows
            part = part + arrived[at : at + rows].astype(F32)
        sent[k * rows : (k + 1) * rows] = part.astype(sent.dtype)


def halve(kept, sent, bits, n):
    rows = kept[0].shape[0]
    got = [swap(sent, bits[-1], n)]
    for bit in bits[-2::-1]:
        upper = kept[len(kept) // 2 :]
        (sent,) = call(
            functools.partial(add_kernel, len(upper)),
            [((len(upper) * rows, kept[0].shape[1]), BF16)],
            [*upper, *got],
        )
        kept = kept[: len(kept) // 2]
        got.append(swap(sent, bit, n))
    return [kept[0], *got], sent


def weights_kernel(ni, nt, row_flips, col_flips, *refs):
    row_parts, refs = refs[: len(row_flips)], refs[len(row_flips) :]
    col_parts, refs = refs[: len(col_flips)], refs[len(col_flips) :]
    raw, last_col, last_row, img_low, txt_low = refs[:5]
    half = ni // 2
    *img_kept, img_sent, weights_bf, inners = refs[5:]
    rows = LANES
    row_lse = merge(row_parts, row_flips)
    col_lse = merge(col_parts, col_flips)
    inner_col = [jnp.zeros((1, rows), F32) for _ in range(nt)]
    for a in range(ni):
        row = column_of(row_lse[a : a + 1])
        inner_row = jnp.zeros((rows, rows), F32)
        for t in range(nt):
            cols = slice(t * rows, (t + 1) * rows)
            if a == ni - 1:
                here = last_row[:, cols]
            else:
                here = (raw[a * rows : (a + 1) * rows, cols] if t < nt - 1 else last_col[a * rows : (a + 1) * rows])
            scores = LOGIT_SCALE * here
            weights = jnp.exp(scores - row) + jnp.exp(scores - col_lse[t : t + 1])
            weights_bf[a * rows : (a + 1) * rows, t * rows : (t + 1) * rows] = weights.astype(BF16)
            weighted = weights * here
            inner_row = inner_row + weighted
            inner_col[t] = inner_col[t] + jnp.sum(weighted, axis=0, keepdims=True)
        inner = jnp.sum(inner_row, axis=1, keepdims=True)
        part = (
            dot(weights_bf[a * rows : (a + 1) * rows], txt_low[...])
            - inner * img_low[a * rows : (a + 1) * rows]
        )
        if a < half:
            img_kept[a][...] = part
        else:
            img_sent[(a - half) * rows : (a - half + 1) * rows] = part.astype(img_sent.dtype)
    for t in range(nt):
        inners[t : t + 1] = inner_col[t]


def columns_kernel(nt, weights_bf, inners, img_side_t, txt_side_t, *refs):
    rows, kept, sent = LANES, refs[:-1], refs[-1]
    for t in range(nt):
        here = slice(t * rows, (t + 1) * rows)
        part = dot(img_side_t[...], weights_bf[:, here]) - inners[t : t + 1] * txt_side_t[:, here]
        if t < nt // 2:
            kept[t][...] = part
        else:
            sent[(t - nt // 2) * rows : (t - nt // 2 + 1) * rows] = part.astype(sent.dtype)


def sketch_kernel(count, turned, *refs):
    parts, (base, keys, out, made, sems) = refs[:count], refs[count:]
    rows = base.shape[0]
    grad = sum((part[:rows].astype(F32) for part in parts[1:]), parts[0][...])
    grad = (grad.T if turned else grad) + base[...]
    copies, step = [], rows // 2
    for k in range(2):
        here = slice(k * step, (k + 1) * step)
        for a in range(0, made.shape[1], LANES):
            made[here, a : a + LANES] = (keys[here, a : a + LANES] * grad[here]).astype(BF16)
        copies.append(pltpu.make_async_copy(made.at[here], out.at[here], sems.at[k]))
        copies[-1].start()
    for copy in copies:
        copy.wait()


def sketch(parts, base, keys, turned):
    args = [pltpu.with_memory_space_constraint(a, pltpu.VMEM) for a in [*parts, base, keys]]
    return pl.pallas_call(
        functools.partial(sketch_kernel, len(parts), turned),
        out_shape=jax.ShapeDtypeStruct(keys.shape, BF16),
        in_specs=[pl.BlockSpec(memory_space=pltpu.VMEM)] * len(args),
        out_specs=pl.BlockSpec(memory_space=pltpu.HBM),
        scratch_shapes=[pltpu.VMEM(keys.shape, BF16), pltpu.SemaphoreType.DMA((2,))],
        compiler_params=pltpu.CompilerParams(vmem_limit_bytes=16 << 20),
        cost_estimate=pl.CostEstimate(flops=keys.size, bytes_accessed=6 * keys.size, transcendentals=0),
    )(*args)


def body(n, img_feats, txt_feats, w_img, w_txt, a_img, b_img, a_txt, b_txt):
    rows, wide = img_feats.shape[0], w_img.shape[1]
    low = b_img.shape[1]
    assert rows == LANES and low == LANES
    img_bits, txt_bits = split_bits(n)
    img_span, txt_span = span(img_bits), span(txt_bits)
    ni, nt = len(img_span), len(txt_span)
    (img_emb,), img_inv = stream_embed([img_feats], w_img, False)
    far = gather(txt_feats, txt_bits[:-1], n)
    near = swap(txt_feats, txt_bits[-1], n)
    (txt_emb,), txt_inv, w_txt_v = stream_embed([txt_feats], w_txt, True)
    far = [txt_emb] + [embed([x], w_txt_v)[0] for x in far[1:]]
    onward = [swap(x, txt_bits[-1], n) for x in far[1:]]
    texts = far + embed([near], w_txt_v) + onward
    img_keys, txt_keys = call(
        keys_kernel,
        [((rows, a_img.shape[1] * LANES), F32), ((rows, a_txt.shape[1] * LANES), F32)],
        [img_feats, txt_feats, a_img.T, a_txt.T, img_inv, txt_inv],
        after=far[1:2],
    )
    images = gather(img_emb, img_bits, n, lambda x: hold(x, [texts[0], img_keys]))
    raw, *halfway = call(
        functools.partial(scores_kernel, ni - 1, nt - 1),
        [(((ni - 1) * rows, (nt - 1) * rows), F32)]
        + [(((ni - 1) * rows, 1), F32)] * 2
        + [((nt - 1, rows), F32)] * 2,
        images[:-1] + texts[:-1],
        scratch=[pltpu.VMEM(((ni - 1) * rows, wide), BF16), pltpu.VMEM(((nt - 1) * rows, wide), BF16)],
        flops=2 * (ni - 1) * (nt - 1) * rows * rows * wide,
    )
    last_col, last_row, row_lse, col_lse = call(
        functools.partial(last_scores_kernel, ni, nt),
        [(((ni - 1) * rows, rows), F32), ((rows, nt * rows), F32), ((ni, rows), F32), ((nt, rows), F32)],
        images + texts + halfway,
        scratch=[pltpu.VMEM(((ni - 1) * rows, wide), BF16), pltpu.VMEM((nt * rows, wide), BF16)],
        flops=2 * (ni + nt) * rows * rows * wide,
    )
    row_parts = gather(row_lse, img_bits, n)
    col_parts, col_flips = gather_lse(col_lse, txt_bits, n)
    img_low, img_side_t, txt_low, txt_side_t, img_base, txt_base = call(
        functools.partial(factors_kernel, ni, nt),
        [
            ((ni * rows, low), F32),
            ((low, ni * rows), BF16),
            ((nt * rows, low), BF16),
            ((low, nt * rows), F32),
            ((rows, low), F32),
            ((rows, low), F32),
        ],
        images + texts + [b_img, b_txt],
        flops=4 * (ni + nt) * rows * wide * low,
    )
    half = ni // 2
    *img_kept, img_sent, weights_bf, inners = call(
        functools.partial(weights_kernel, ni, nt, tuple(range(ni)), col_flips),
        [((rows, low), F32)] * half
        + [((half * rows, low), BF16), ((ni * rows, nt * rows), BF16), ((nt, rows), F32)],
        row_parts + col_parts + [raw, last_col, last_row, img_low, txt_low],
        flops=2 * ni * nt * rows * rows * low,
    )
    *txt_kept, txt_sent = call(
        functools.partial(columns_kernel, nt),
        [((rows, low), F32)] * (nt // 2) + [((nt // 2 * rows, low), BF16)],
        [weights_bf, inners, img_side_t, txt_side_t],
        flops=2 * ni * nt * rows * rows * low,
    )
    img_parts, _ = halve(img_kept, img_sent, img_bits, n)
    txt_parts, _ = halve(txt_kept, txt_sent, txt_bits, n)
    return (
        sketch(img_parts, img_base, img_keys, False),
        sketch(txt_parts, txt_base, txt_keys, True),
    )


def solution(mesh):
    n = mesh.shape["dp"]
    rows = P(("ckpt", "dp"), None)
    part = P("ckpt", None)
    return jax.shard_map(
        lambda *args: body(n, *args),
        mesh=mesh,
        in_specs=(rows, rows, part, part, P(), P(), P(), P()),
        out_specs=(rows, rows),
        check_vma=False,
    )
```

```python
import functools
import jax
import jax.numpy as jnp
from jax import lax
from jax.experimental import pallas as pl
from jax.experimental.pallas import tpu as pltpu
from jax.sharding import PartitionSpec as P

LOGIT_SCALE = 100.0
EPSILON = 1e-06
F32 = jnp.float32
BF16 = jnp.bfloat16
LANES = 128
PIECES = 4


def dot(left, right, left_dim=1, right_dim=0):
    return lax.dot_general(
        left, right, (((left_dim,), (right_dim,)), ((), ())), preferred_element_type=F32
    )


def skip(kernel, first, count, *refs):
    kernel(*refs[:first], *refs[first + count :])


def call(kernel, outs, args, after=(), free=(), scratch=(), flops=0, limit=16):
    args = [a if k in free else pltpu.with_memory_space_constraint(a, pltpu.VMEM) for k, a in enumerate(args)]
    size = sum(a.size * a.dtype.itemsize for a in args)
    specs = [pl.BlockSpec(memory_space=pltpu.VMEM)] * len(args)
    if after:
        kernel = functools.partial(skip, kernel, len(args), len(after))
        args += [pltpu.with_memory_space_constraint(a, pltpu.VMEM) for a in after]
        specs += [pl.BlockSpec(memory_space=pltpu.VMEM)] * len(after)
    return pl.pallas_call(
        kernel,
        out_shape=[jax.ShapeDtypeStruct(s, d) for s, d in outs],
        in_specs=specs,
        out_specs=[pl.BlockSpec(memory_space=pltpu.VMEM)] * len(outs),
        scratch_shapes=list(scratch),
        compiler_params=pltpu.CompilerParams(vmem_limit_bytes=limit << 20),
        cost_estimate=pl.CostEstimate(flops=flops, bytes_accessed=size, transcendentals=0),
    )(*args)


def span(bits):
    offsets = [0]
    for bit in bits:
        offsets = offsets + [o ^ bit for o in offsets]
    return offsets


def split_bits(n):
    bits = [1 << b for b in range(n.bit_length() - 1)]
    assert 1 << len(bits) == n
    half = len(bits) // 2
    return bits[:half:-1] + bits[:1], bits[half:0:-1]


def swap(x, offset, n):
    return lax.ppermute(x, "dp", [(i, i ^ offset) for i in range(n)])


def gather(block, bits, n, ready=None):
    blocks = [block]
    for bit in bits:
        new = [swap(b, bit, n) for b in blocks]
        blocks = blocks + (new if ready is None or bit == bits[-1] else [ready(b) for b in new])
    return blocks


def normalised(raw):
    inverse = lax.rsqrt(jnp.sum(raw * raw, axis=1, keepdims=True) + EPSILON)
    return (raw * inverse).astype(BF16), inverse


def embed_kernel(blocks, *refs):
    feats, weight, embs = refs[:blocks], refs[blocks], refs[blocks + 1 :]
    for b in range(blocks):
        embs[b][...] = normalised(dot(feats[b][...], weight[...]))[0]


def embed(feats, weight):
    rows, blocks = feats[0].shape[0], len(feats)
    return list(
        call(
            functools.partial(embed_kernel, blocks),
            [((rows, weight.shape[1]), BF16)] * blocks,
            [*feats, weight],
            flops=2 * blocks * rows * weight.size,
        )
    )


def stream_kernel(blocks, cuts, *refs):
    feats, weight, embs = refs[:blocks], refs[blocks], refs[blocks + 1 : 2 * blocks + 1]
    inverse, weight_v, own_v, sems = refs[2 * blocks + 1 :]
    own = pltpu.make_async_copy(feats[0], own_v, sems.at[0])
    pieces = [slice(lo, hi) for lo, hi in zip(cuts, cuts[1:])]
    copies = [
        pltpu.make_async_copy(weight.at[p], weight_v.at[p], sems.at[1 + k]) for k, p in enumerate(pieces)
    ]
    for copy in [own, *copies]:
        copy.start()
    own.wait()
    raws = [0.0] * blocks
    for p, copy in zip(pieces, copies):
        copy.wait()
        for b in range(blocks):
            left = own_v[:, p] if b == 0 else feats[b][:, p]
            raws[b] = raws[b] + dot(left, weight_v[p])
    embs[0][...], inverse[...] = normalised(raws[0])
    for b in range(1, blocks):
        embs[b][...] = normalised(raws[b])[0]


def stream_embed(feats, weight, keep):
    (rows, depth), blocks = feats[0].shape, len(feats)
    cuts = [depth // LANES * k // PIECES * LANES for k in range(PIECES)] + [depth]
    far = [pltpu.with_memory_space_constraint(a, pltpu.HBM) for a in (feats[0], weight)]
    near = [pltpu.with_memory_space_constraint(a, pltpu.VMEM) for a in feats[1:]]
    hbm, vmem = pl.BlockSpec(memory_space=pltpu.HBM), pl.BlockSpec(memory_space=pltpu.VMEM)
    outs = [((rows, weight.shape[1]), BF16)] * blocks + [((rows, 1), F32)] + [(weight.shape, BF16)] * keep
    out = pl.pallas_call(
        functools.partial(stream_kernel, blocks, cuts),
        out_shape=[jax.ShapeDtypeStruct(*o) for o in outs],
        in_specs=[hbm] + [vmem] * (blocks - 1) + [hbm],
        out_specs=[vmem] * len(outs),
        scratch_shapes=[pltpu.VMEM(weight.shape, BF16)] * (not keep)
        + [pltpu.VMEM((rows, depth), BF16), pltpu.SemaphoreType.DMA((PIECES + 1,))],
        compiler_params=pltpu.CompilerParams(vmem_limit_bytes=16 << 20),
        cost_estimate=pl.CostEstimate(
            flops=2 * blocks * rows * weight.size, bytes_accessed=2 * weight.size, transcendentals=0
        ),
    )(far[0], *near, far[1])
    return list(out[:blocks]), *out[blocks:]


def keys_kernel(*refs):
    for feats, factor, inverse, wide in zip(refs[:2], refs[2:4], refs[4:6], refs[6:8]):
        keys = dot(feats[...], factor[...], 1, 1) * inverse[...]
        for a in range(keys.shape[1]):
            wide[:, a * LANES : (a + 1) * LANES] = jnp.broadcast_to(keys[:, a : a + 1], (keys.shape[0], LANES))


def hold(x, after):
    args = [pltpu.with_memory_space_constraint(a, pltpu.VMEM) for a in [x, *after]]
    return pl.pallas_call(
        lambda *refs: None,
        out_shape=jax.ShapeDtypeStruct(x.shape, x.dtype),
        in_specs=[pl.BlockSpec(memory_space=pltpu.VMEM)] * len(args),
        out_specs=pl.BlockSpec(memory_space=pltpu.VMEM),
        input_output_aliases={0: 0},
        compiler_params=pltpu.CompilerParams(vmem_limit_bytes=1 << 20),
    )(*args)


def column_of(row):
    return jnp.broadcast_to(row, (LANES, LANES)).T


def lse_parts(scores, axis):
    top = jnp.max(scores, axis=axis, keepdims=True)
    return top, jnp.sum(jnp.exp(scores - top), axis=axis, keepdims=True)


def lay(blocks, whole):
    rows = blocks[0].shape[0]
    for k, block in enumerate(blocks):
        whole[k * rows : (k + 1) * rows] = block[...]


def scores_kernel(ni, nt, *refs):
    images, texts, refs = refs[:ni], refs[ni : ni + nt], refs[ni + nt :]
    raw, row_top, row_total, col_top, col_total, all_images, all_texts = refs
    rows = images[0].shape[0]
    lay(images, all_images)
    lay(texts, all_texts)
    raw[...] = dot(all_images[...], all_texts[...], 1, 1)
    row_top[...], row_total[...] = lse_parts(LOGIT_SCALE * raw[...], 1)
    for t in range(nt):
        col_top[t : t + 1], col_total[t : t + 1] = lse_parts(LOGIT_SCALE * raw[:, t * rows : (t + 1) * rows], 0)


def joined(top, total, other_top, other_total):
    high = jnp.maximum(top, other_top)
    return high + jnp.log(total * jnp.exp(top - high) + other_total * jnp.exp(other_top - high))


def last_scores_kernel(ni, nt, *refs):
    image, text, row_top, row_total, col_top, col_total, all_images, all_texts, *refs = refs
    last_col, last_row, row_lse, col_lse = refs
    rows = image.shape[0]
    last_col[...] = dot(all_images[...], text[...], 1, 1)
    last_row[:, : (nt - 1) * rows] = dot(image[...], all_texts[...], 1, 1)
    last_row[:, (nt - 1) * rows :] = dot(image[...], text[...], 1, 1)
    col_scores, row_scores = LOGIT_SCALE * last_col[...], LOGIT_SCALE * last_row[...]
    lse = joined(row_top[...], row_total[...], *lse_parts(col_scores, 1))
    top, total = lse_parts(row_scores, 1)
    lses = [lse[a * rows : (a + 1) * rows] for a in range(ni - 1)] + [top + jnp.log(total)]
    for a in range(ni):
        row_lse[a : a + 1] = jnp.broadcast_to(lses[a], (rows, LANES)).T[:1]
    for t in range(nt):
        top, total = lse_parts(row_scores[:, t * rows : (t + 1) * rows], 0)
        if t < nt - 1:
            others = col_top[t : t + 1], col_total[t : t + 1]
        else:
            others = lse_parts(col_scores, 0)
        col_lse[t : t + 1] = joined(top, total, *others)


def factors_kernel(ni, nt, *refs):
    images, texts, (b_img, b_txt) = refs[:ni], refs[ni : ni + nt], refs[ni + nt : ni + nt + 2]
    img_low, img_side_t, txt_low, txt_side_t, img_base, txt_base = refs[ni + nt + 2 :]
    rows = images[0].shape[0]
    for a in range(ni):
        here = slice(a * rows, (a + 1) * rows)
        low = dot(images[a][...], b_img[...])
        side = dot(images[a][...], b_txt[...])
        img_low[here] = low
        img_side_t[:, here] = side.T.astype(BF16)
        if a == 0:
            own_img_low, own_img_side = low, side.astype(BF16).astype(F32)
    for t in range(nt):
        here = slice(t * rows, (t + 1) * rows)
        low = dot(texts[t][...], b_img[...]).astype(BF16)
        side = dot(texts[t][...], b_txt[...])
        txt_low[here] = low
        txt_side_t[:, here] = side.T
        if t == 0:
            own_txt_low, own_txt_side = low.astype(F32), side
    diagonal = jnp.sum(
        images[0][...].astype(F32) * texts[0][...].astype(F32), axis=1, keepdims=True
    )
    img_base[...] = 2.0 * (diagonal * own_img_low - own_txt_low)
    txt_base[...] = 2.0 * (diagonal * own_txt_side - own_img_side)


def merge(parts, flips):
    slots = parts[0].shape[0]
    lined = [parts[0][...]]
    for k in range(1, len(parts)):
        lined.append(
            jnp.concatenate([parts[k][s ^ flips[k] :][:1] for s in range(slots)], axis=0)
        )
    top = functools.reduce(jnp.maximum, lined)
    return top + jnp.log(sum(jnp.exp(p - top) for p in lined))


def merge_kernel(flips, *refs):
    refs[-1][...] = merge(refs[:-1], flips)


def gather_lse(lse, bits, n):
    for j, bit in enumerate(bits[:-1]):
        (lse,) = call(functools.partial(merge_kernel, (0, 1 << j)), [(lse.shape, F32)], [lse, swap(lse, bit, n)])
    return [lse, swap(lse, bits[-1], n)], (0, 1 << len(bits) - 1)


def add_kernel(count, *refs):
    own, got, sent = refs[:count], refs[count:-1], refs[-1]
    rows = own[0].shape[0]
    for k in range(count):
        part = own[k][...]
        for arrived in got:
            at = (count + k) * rows
            part = part + arrived[at : at + rows].astype(F32)
        sent[k * rows : (k + 1) * rows] = part.astype(sent.dtype)


def halve(kept, sent, bits, n):
    rows = kept[0].shape[0]
    got = [swap(sent, bits[-1], n)]
    for bit in bits[-2::-1]:
        upper = kept[len(kept) // 2 :]
        (sent,) = call(
            functools.partial(add_kernel, len(upper)),
            [((len(upper) * rows, kept[0].shape[1]), BF16)],
            [*upper, *got],
        )
        kept = kept[: len(kept) // 2]
        got.append(swap(sent, bit, n))
    return [kept[0], *got], sent


def weights_kernel(ni, nt, row_flips, col_flips, *refs):
    row_parts, refs = refs[: len(row_flips)], refs[len(row_flips) :]
    col_parts, refs = refs[: len(col_flips)], refs[len(col_flips) :]
    raw, last_col, last_row, img_low, txt_low = refs[:5]
    half = ni // 2
    *img_kept, img_sent, weights_bf, inners = refs[5:]
    rows = LANES
    row_lse = merge(row_parts, row_flips)
    col_lse = merge(col_parts, col_flips)
    inner_col = [jnp.zeros((1, rows), F32) for _ in range(nt)]
    for a in range(ni):
        row = column_of(row_lse[a : a + 1])
        inner_row = jnp.zeros((rows, rows), F32)
        for t in range(nt):
            cols = slice(t * rows, (t + 1) * rows)
            if a == ni - 1:
                here = last_row[:, cols]
            else:
                here = (raw[a * rows : (a + 1) * rows, cols] if t < nt - 1 else last_col[a * rows : (a + 1) * rows])
            scores = LOGIT_SCALE * here
            weights = jnp.exp(scores - row) + jnp.exp(scores - col_lse[t : t + 1])
            weights_bf[a * rows : (a + 1) * rows, t * rows : (t + 1) * rows] = weights.astype(BF16)
            weighted = weights * here
            inner_row = inner_row + weighted
            inner_col[t] = inner_col[t] + jnp.sum(weighted, axis=0, keepdims=True)
        inner = jnp.sum(inner_row, axis=1, keepdims=True)
        part = (
            dot(weights_bf[a * rows : (a + 1) * rows], txt_low[...])
            - inner * img_low[a * rows : (a + 1) * rows]
        )
        if a < half:
            img_kept[a][...] = part
        else:
            img_sent[(a - half) * rows : (a - half + 1) * rows] = part.astype(img_sent.dtype)
    for t in range(nt):
        inners[t : t + 1] = inner_col[t]


def columns_kernel(nt, weights_bf, inners, img_side_t, txt_side_t, *refs):
    rows, kept, sent = LANES, refs[:-1], refs[-1]
    for t in range(nt):
        here = slice(t * rows, (t + 1) * rows)
        part = dot(img_side_t[...], weights_bf[:, here]) - inners[t : t + 1] * txt_side_t[:, here]
        if t < nt // 2:
            kept[t][...] = part
        else:
            sent[(t - nt // 2) * rows : (t - nt // 2 + 1) * rows] = part.astype(sent.dtype)


def sketch_kernel(count, turned, *refs):
    parts, (base, keys, out, made, sems) = refs[:count], refs[count:]
    rows = base.shape[0]
    grad = sum((part[:rows].astype(F32) for part in parts[1:]), parts[0][...])
    grad = (grad.T if turned else grad) + base[...]
    copies, step = [], rows // 2
    for k in range(2):
        here = slice(k * step, (k + 1) * step)
        for a in range(0, made.shape[1], LANES):
            made[here, a : a + LANES] = (keys[here, a : a + LANES] * grad[here]).astype(BF16)
        copies.append(pltpu.make_async_copy(made.at[here], out.at[here], sems.at[k]))
        copies[-1].start()
    for copy in copies:
        copy.wait()


def sketch(parts, base, keys, turned):
    args = [pltpu.with_memory_space_constraint(a, pltpu.VMEM) for a in [*parts, base, keys]]
    return pl.pallas_call(
        functools.partial(sketch_kernel, len(parts), turned),
        out_shape=jax.ShapeDtypeStruct(keys.shape, BF16),
        in_specs=[pl.BlockSpec(memory_space=pltpu.VMEM)] * len(args),
        out_specs=pl.BlockSpec(memory_space=pltpu.HBM),
        scratch_shapes=[pltpu.VMEM(keys.shape, BF16), pltpu.SemaphoreType.DMA((2,))],
        compiler_params=pltpu.CompilerParams(vmem_limit_bytes=16 << 20),
        cost_estimate=pl.CostEstimate(flops=keys.size, bytes_accessed=6 * keys.size, transcendentals=0),
    )(*args)


def body(n, img_feats, txt_feats, w_img, w_txt, a_img, b_img, a_txt, b_txt):
    rows, wide = img_feats.shape[0], w_img.shape[1]
    low = b_img.shape[1]
    assert rows == LANES and low == LANES
    img_bits, txt_bits = split_bits(n)
    img_span, txt_span = span(img_bits), span(txt_bits)
    ni, nt = len(img_span), len(txt_span)
    (img_emb,), img_inv = stream_embed([img_feats], w_img, False)
    far = gather(txt_feats, txt_bits[:-1], n)
    near = swap(txt_feats, txt_bits[-1], n)
    (txt_emb,), txt_inv, w_txt_v = stream_embed([txt_feats], w_txt, True)
    far = [txt_emb] + [embed([x], w_txt_v)[0] for x in far[1:]]
    onward = [swap(x, txt_bits[-1], n) for x in far[1:]]
    texts = far + embed([near], w_txt_v) + onward
    img_keys, txt_keys = call(
        keys_kernel,
        [((rows, a_img.shape[1] * LANES), F32), ((rows, a_txt.shape[1] * LANES), F32)],
        [img_feats, txt_feats, a_img.T, a_txt.T, img_inv, txt_inv],
        after=far[1:2],
    )
    images = gather(img_emb, img_bits, n, lambda x: hold(x, [texts[0], img_keys]))
    raw, *halfway = call(
        functools.partial(scores_kernel, ni - 1, nt - 1),
        [(((ni - 1) * rows, (nt - 1) * rows), F32)]
        + [(((ni - 1) * rows, 1), F32)] * 2
        + [((nt - 1, rows), F32)] * 2
        + [(((ni - 1) * rows, wide), BF16), (((nt - 1) * rows, wide), BF16)],
        images[:-1] + texts[:-1],
        flops=2 * (ni - 1) * (nt - 1) * rows * rows * wide,
    )
    last_col, last_row, row_lse, col_lse = call(
        functools.partial(last_scores_kernel, ni, nt),
        [(((ni - 1) * rows, rows), F32), ((rows, nt * rows), F32), ((ni, rows), F32), ((nt, rows), F32)],
        [images[-1], texts[-1], *halfway],
        flops=2 * (ni + nt) * rows * rows * wide,
    )
    row_parts = gather(row_lse, img_bits, n)
    col_parts, col_flips = gather_lse(col_lse, txt_bits, n)
    img_low, img_side_t, txt_low, txt_side_t, img_base, txt_base = call(
        functools.partial(factors_kernel, ni, nt),
        [
            ((ni * rows, low), F32),
            ((low, ni * rows), BF16),
            ((nt * rows, low), BF16),
            ((low, nt * rows), F32),
            ((rows, low), F32),
            ((rows, low), F32),
        ],
        images + texts + [b_img, b_txt],
        flops=4 * (ni + nt) * rows * wide * low,
    )
    half = ni // 2
    *img_kept, img_sent, weights_bf, inners = call(
        functools.partial(weights_kernel, ni, nt, tuple(range(ni)), col_flips),
        [((rows, low), F32)] * half
        + [((half * rows, low), BF16), ((ni * rows, nt * rows), BF16), ((nt, rows), F32)],
        row_parts + col_parts + [raw, last_col, last_row, img_low, txt_low],
        flops=2 * ni * nt * rows * rows * low,
    )
    *txt_kept, txt_sent = call(
        functools.partial(columns_kernel, nt),
        [((rows, low), F32)] * (nt // 2) + [((nt // 2 * rows, low), BF16)],
        [weights_bf, inners, img_side_t, txt_side_t],
        flops=2 * ni * nt * rows * rows * low,
    )
    img_parts, _ = halve(img_kept, img_sent, img_bits, n)
    txt_parts, _ = halve(txt_kept, txt_sent, txt_bits, n)
    return (
        sketch(img_parts, img_base, img_keys, False),
        sketch(txt_parts, txt_base, txt_keys, True),
    )


def solution(mesh):
    n = mesh.shape["dp"]
    rows = P(("ckpt", "dp"), None)
    part = P("ckpt", None)
    return jax.shard_map(
        lambda *args: body(n, *args),
        mesh=mesh,
        in_specs=(rows, rows, part, part, P(), P(), P(), P()),
        out_specs=(rows, rows),
        check_vma=False,
    )
```

```python
import functools
import jax
import jax.numpy as jnp
from jax import lax
from jax.experimental import pallas as pl
from jax.experimental.pallas import tpu as pltpu
from jax.sharding import PartitionSpec as P

LOGIT_SCALE = 100.0
EPSILON = 1e-06
F32 = jnp.float32
BF16 = jnp.bfloat16
LANES = 128
PIECES = 4


def dot(left, right, left_dim=1, right_dim=0):
    return lax.dot_general(
        left, right, (((left_dim,), (right_dim,)), ((), ())), preferred_element_type=F32
    )


def skip(kernel, first, count, *refs):
    kernel(*refs[:first], *refs[first + count :])


def call(kernel, outs, args, after=(), free=(), scratch=(), flops=0, limit=16):
    args = [a if k in free else pltpu.with_memory_space_constraint(a, pltpu.VMEM) for k, a in enumerate(args)]
    size = sum(a.size * a.dtype.itemsize for a in args)
    specs = [pl.BlockSpec(memory_space=pltpu.VMEM)] * len(args)
    if after:
        kernel = functools.partial(skip, kernel, len(args), len(after))
        args += [pltpu.with_memory_space_constraint(a, pltpu.VMEM) for a in after]
        specs += [pl.BlockSpec(memory_space=pltpu.VMEM)] * len(after)
    return pl.pallas_call(
        kernel,
        out_shape=[jax.ShapeDtypeStruct(s, d) for s, d in outs],
        in_specs=specs,
        out_specs=[pl.BlockSpec(memory_space=pltpu.VMEM)] * len(outs),
        scratch_shapes=list(scratch),
        compiler_params=pltpu.CompilerParams(vmem_limit_bytes=limit << 20),
        cost_estimate=pl.CostEstimate(flops=flops, bytes_accessed=size, transcendentals=0),
    )(*args)


def span(bits):
    offsets = [0]
    for bit in bits:
        offsets = offsets + [o ^ bit for o in offsets]
    return offsets


def split_bits(n):
    bits = [1 << b for b in range(n.bit_length() - 1)]
    assert 1 << len(bits) == n
    half = len(bits) // 2
    return bits[:half:-1] + bits[:1], bits[half:0:-1]


def swap(x, offset, n):
    return lax.ppermute(x, "dp", [(i, i ^ offset) for i in range(n)])


def gather(block, bits, n, ready=None):
    blocks = [block]
    for bit in bits:
        new = [swap(b, bit, n) for b in blocks]
        blocks = blocks + (new if ready is None or bit == bits[-1] else [ready(b) for b in new])
    return blocks


def normalised(raw):
    inverse = lax.rsqrt(jnp.sum(raw * raw, axis=1, keepdims=True) + EPSILON)
    return (raw * inverse).astype(BF16), inverse


def embed_kernel(blocks, *refs):
    feats, weight, embs = refs[:blocks], refs[blocks], refs[blocks + 1 :]
    for b in range(blocks):
        embs[b][...] = normalised(dot(feats[b][...], weight[...]))[0]


def embed(feats, weight):
    rows, blocks = feats[0].shape[0], len(feats)
    return list(
        call(
            functools.partial(embed_kernel, blocks),
            [((rows, weight.shape[1]), BF16)] * blocks,
            [*feats, weight],
            flops=2 * blocks * rows * weight.size,
        )
    )


def stream_kernel(blocks, cuts, *refs):
    feats, weight, embs = refs[:blocks], refs[blocks], refs[blocks + 1 : 2 * blocks + 1]
    inverse, weight_v, own_v, sems = refs[2 * blocks + 1 :]
    own = pltpu.make_async_copy(feats[0], own_v, sems.at[0])
    pieces = [slice(lo, hi) for lo, hi in zip(cuts, cuts[1:])]
    copies = [
        pltpu.make_async_copy(weight.at[p], weight_v.at[p], sems.at[1 + k]) for k, p in enumerate(pieces)
    ]
    for copy in [own, *copies]:
        copy.start()
    own.wait()
    raws = [0.0] * blocks
    for p, copy in zip(pieces, copies):
        copy.wait()
        for b in range(blocks):
            left = own_v[:, p] if b == 0 else feats[b][:, p]
            raws[b] = raws[b] + dot(left, weight_v[p])
    embs[0][...], inverse[...] = normalised(raws[0])
    for b in range(1, blocks):
        embs[b][...] = normalised(raws[b])[0]


def stream_embed(feats, weight, keep):
    (rows, depth), blocks = feats[0].shape, len(feats)
    cuts = [depth // LANES * k // PIECES * LANES for k in range(PIECES)] + [depth]
    far = [pltpu.with_memory_space_constraint(a, pltpu.HBM) for a in (feats[0], weight)]
    near = [pltpu.with_memory_space_constraint(a, pltpu.VMEM) for a in feats[1:]]
    hbm, vmem = pl.BlockSpec(memory_space=pltpu.HBM), pl.BlockSpec(memory_space=pltpu.VMEM)
    outs = [((rows, weight.shape[1]), BF16)] * blocks + [((rows, 1), F32)] + [(weight.shape, BF16)] * keep
    out = pl.pallas_call(
        functools.partial(stream_kernel, blocks, cuts),
        out_shape=[jax.ShapeDtypeStruct(*o) for o in outs],
        in_specs=[hbm] + [vmem] * (blocks - 1) + [hbm],
        out_specs=[vmem] * len(outs),
        scratch_shapes=[pltpu.VMEM(weight.shape, BF16)] * (not keep)
        + [pltpu.VMEM((rows, depth), BF16), pltpu.SemaphoreType.DMA((PIECES + 1,))],
        compiler_params=pltpu.CompilerParams(vmem_limit_bytes=16 << 20),
        cost_estimate=pl.CostEstimate(
            flops=2 * blocks * rows * weight.size, bytes_accessed=2 * weight.size, transcendentals=0
        ),
    )(far[0], *near, far[1])
    return list(out[:blocks]), *out[blocks:]


def keys_kernel(*refs):
    for feats, factor, inverse, wide in zip(refs[:2], refs[2:4], refs[4:6], refs[6:8]):
        keys = dot(feats[...], factor[...], 1, 1) * inverse[...]
        for a in range(keys.shape[1]):
            wide[:, a * LANES : (a + 1) * LANES] = jnp.broadcast_to(keys[:, a : a + 1], (keys.shape[0], LANES))


def hold(x, after):
    args = [pltpu.with_memory_space_constraint(a, pltpu.VMEM) for a in [x, *after]]
    return pl.pallas_call(
        lambda *refs: None,
        out_shape=jax.ShapeDtypeStruct(x.shape, x.dtype),
        in_specs=[pl.BlockSpec(memory_space=pltpu.VMEM)] * len(args),
        out_specs=pl.BlockSpec(memory_space=pltpu.VMEM),
        input_output_aliases={0: 0},
        compiler_params=pltpu.CompilerParams(vmem_limit_bytes=1 << 20),
    )(*args)


def column_of(row):
    return jnp.broadcast_to(row, (LANES, LANES)).T


def lse_parts(scores, axis):
    top = jnp.max(scores, axis=axis, keepdims=True)
    return top, jnp.sum(jnp.exp(scores - top), axis=axis, keepdims=True)


def lay(blocks, whole):
    rows = blocks[0].shape[0]
    for k, block in enumerate(blocks):
        whole[k * rows : (k + 1) * rows] = block[...]


def scores_kernel(ni, nt, *refs):
    images, texts, refs = refs[:ni], refs[ni : ni + nt], refs[ni + nt :]
    raw, row_top, row_total, col_top, col_total, all_images, all_texts = refs
    rows = images[0].shape[0]
    lay(images, all_images)
    lay(texts, all_texts)
    raw[...] = dot(all_images[...], all_texts[...], 1, 1)
    row_top[...], row_total[...] = lse_parts(LOGIT_SCALE * raw[...], 1)
    for t in range(nt):
        col_top[t : t + 1], col_total[t : t + 1] = lse_parts(LOGIT_SCALE * raw[:, t * rows : (t + 1) * rows], 0)


def joined(top, total, other_top, other_total):
    high = jnp.maximum(top, other_top)
    return high + jnp.log(total * jnp.exp(top - high) + other_total * jnp.exp(other_top - high))


def last_scores_kernel(ni, nt, *refs):
    images, texts, refs = refs[:ni], refs[ni : ni + nt], refs[ni + nt :]
    row_top, row_total, col_top, col_total, last_col, last_row, row_lse, col_lse, all_images, all_texts = refs
    rows = images[0].shape[0]
    lay(images[:-1], all_images)
    lay(texts, all_texts)
    last_col[...] = dot(all_images[...], texts[-1][...], 1, 1)
    last_row[...] = dot(images[-1][...], all_texts[...], 1, 1)
    col_scores, row_scores = LOGIT_SCALE * last_col[...], LOGIT_SCALE * last_row[...]
    lse = joined(row_top[...], row_total[...], *lse_parts(col_scores, 1))
    top, total = lse_parts(row_scores, 1)
    lses = [lse[a * rows : (a + 1) * rows] for a in range(ni - 1)] + [top + jnp.log(total)]
    for a in range(ni):
        row_lse[a : a + 1] = jnp.broadcast_to(lses[a], (rows, LANES)).T[:1]
    for t in range(nt):
        top, total = lse_parts(row_scores[:, t * rows : (t + 1) * rows], 0)
        if t < nt - 1:
            others = col_top[t : t + 1], col_total[t : t + 1]
        else:
            others = lse_parts(col_scores, 0)
        col_lse[t : t + 1] = joined(top, total, *others)


def factors_kernel(ni, nt, *refs):
    images, texts, (b_img, b_txt) = refs[:ni], refs[ni : ni + nt], refs[ni + nt : ni + nt + 2]
    img_low, img_side_t, txt_low, txt_side_t, img_base, txt_base = refs[ni + nt + 2 :]
    rows = images[0].shape[0]
    for a in range(ni):
        here = slice(a * rows, (a + 1) * rows)
        low = dot(images[a][...], b_img[...])
        side = dot(images[a][...], b_txt[...])
        img_low[here] = low
        img_side_t[:, here] = side.T.astype(BF16)
        if a == 0:
            own_img_low, own_img_side = low, side.astype(BF16).astype(F32)
    for t in range(nt):
        here = slice(t * rows, (t + 1) * rows)
        low = dot(texts[t][...], b_img[...]).astype(BF16)
        side = dot(texts[t][...], b_txt[...])
        txt_low[here] = low
        txt_side_t[:, here] = side.T
        if t == 0:
            own_txt_low, own_txt_side = low.astype(F32), side
    diagonal = jnp.sum(
        images[0][...].astype(F32) * texts[0][...].astype(F32), axis=1, keepdims=True
    )
    img_base[...] = 2.0 * (diagonal * own_img_low - own_txt_low)
    txt_base[...] = 2.0 * (diagonal * own_txt_side - own_img_side)


def merge(parts, flips):
    slots = parts[0].shape[0]
    lined = [parts[0][...]]
    for k in range(1, len(parts)):
        lined.append(
            jnp.concatenate([parts[k][s ^ flips[k] :][:1] for s in range(slots)], axis=0)
        )
    top = functools.reduce(jnp.maximum, lined)
    return top + jnp.log(sum(jnp.exp(p - top) for p in lined))


def merge_kernel(flips, *refs):
    refs[-1][...] = merge(refs[:-1], flips)


def gather_lse(lse, bits, n):
    for j, bit in enumerate(bits[:-1]):
        (lse,) = call(functools.partial(merge_kernel, (0, 1 << j)), [(lse.shape, F32)], [lse, swap(lse, bit, n)])
    return [lse, swap(lse, bits[-1], n)], (0, 1 << len(bits) - 1)


def add_kernel(count, *refs):
    own, got, sent = refs[:count], refs[count:-1], refs[-1]
    rows = own[0].shape[0]
    for k in range(count):
        part = own[k][...]
        for arrived in got:
            at = (count + k) * rows
            part = part + arrived[at : at + rows].astype(F32)
        sent[k * rows : (k + 1) * rows] = part.astype(sent.dtype)


def halve(kept, sent, bits, n):
    rows = kept[0].shape[0]
    got = [swap(sent, bits[-1], n)]
    for bit in bits[-2::-1]:
        upper = kept[len(kept) // 2 :]
        (sent,) = call(
            functools.partial(add_kernel, len(upper)),
            [((len(upper) * rows, kept[0].shape[1]), BF16)],
            [*upper, *got],
        )
        kept = kept[: len(kept) // 2]
        got.append(swap(sent, bit, n))
    return [kept[0], *got], sent


def weights_kernel(ni, nt, row_flips, col_flips, *refs):
    row_parts, refs = refs[: len(row_flips)], refs[len(row_flips) :]
    col_parts, refs = refs[: len(col_flips)], refs[len(col_flips) :]
    raw, last_col, last_row, img_low, txt_low = refs[:5]
    half = ni // 2
    *img_kept, img_sent, weights_bf, inners = refs[5:]
    rows = LANES
    row_lse = merge(row_parts, row_flips)
    col_lse = merge(col_parts, col_flips)
    inner_col = [jnp.zeros((1, rows), F32) for _ in range(nt)]
    for a in range(ni):
        row = column_of(row_lse[a : a + 1])
        inner_row = jnp.zeros((rows, rows), F32)
        for t in range(nt):
            cols = slice(t * rows, (t + 1) * rows)
            if a == ni - 1:
                here = last_row[:, cols]
            else:
                here = (raw[a * rows : (a + 1) * rows, cols] if t < nt - 1 else last_col[a * rows : (a + 1) * rows])
            scores = LOGIT_SCALE * here
            weights = jnp.exp(scores - row) + jnp.exp(scores - col_lse[t : t + 1])
            weights_bf[a * rows : (a + 1) * rows, t * rows : (t + 1) * rows] = weights.astype(BF16)
            weighted = weights * here
            inner_row = inner_row + weighted
            inner_col[t] = inner_col[t] + jnp.sum(weighted, axis=0, keepdims=True)
        inner = jnp.sum(inner_row, axis=1, keepdims=True)
        part = (
            dot(weights_bf[a * rows : (a + 1) * rows], txt_low[...])
            - inner * img_low[a * rows : (a + 1) * rows]
        )
        if a < half:
            img_kept[a][...] = part
        else:
            img_sent[(a - half) * rows : (a - half + 1) * rows] = part.astype(img_sent.dtype)
    for t in range(nt):
        inners[t : t + 1] = inner_col[t]


def columns_kernel(nt, weights_bf, inners, img_side_t, txt_side_t, *refs):
    rows, kept, sent = LANES, refs[:-1], refs[-1]
    for t in range(nt):
        here = slice(t * rows, (t + 1) * rows)
        part = dot(img_side_t[...], weights_bf[:, here]) - inners[t : t + 1] * txt_side_t[:, here]
        if t < nt // 2:
            kept[t][...] = part
        else:
            sent[(t - nt // 2) * rows : (t - nt // 2 + 1) * rows] = part.astype(sent.dtype)


def sketch_kernel(count, turned, *refs):
    parts, (base, keys, out, made, sems) = refs[:count], refs[count:]
    rows = base.shape[0]
    grad = sum((part[:rows].astype(F32) for part in parts[1:]), parts[0][...])
    grad = (grad.T if turned else grad) + base[...]
    copies, step = [], rows // 4
    for k in range(4):
        here = slice(k * step, (k + 1) * step)
        for a in range(0, made.shape[1], LANES):
            made[here, a : a + LANES] = (keys[here, a : a + LANES] * grad[here]).astype(BF16)
        copies.append(pltpu.make_async_copy(made.at[here], out.at[here], sems.at[k]))
        copies[-1].start()
    for copy in copies:
        copy.wait()


def sketch(parts, base, keys, turned):
    args = [pltpu.with_memory_space_constraint(a, pltpu.VMEM) for a in [*parts, base, keys]]
    return pl.pallas_call(
        functools.partial(sketch_kernel, len(parts), turned),
        out_shape=jax.ShapeDtypeStruct(keys.shape, BF16),
        in_specs=[pl.BlockSpec(memory_space=pltpu.VMEM)] * len(args),
        out_specs=pl.BlockSpec(memory_space=pltpu.HBM),
        scratch_shapes=[pltpu.VMEM(keys.shape, BF16), pltpu.SemaphoreType.DMA((4,))],
        compiler_params=pltpu.CompilerParams(vmem_limit_bytes=16 << 20),
        cost_estimate=pl.CostEstimate(flops=keys.size, bytes_accessed=6 * keys.size, transcendentals=0),
    )(*args)


def body(n, img_feats, txt_feats, w_img, w_txt, a_img, b_img, a_txt, b_txt):
    rows, wide = img_feats.shape[0], w_img.shape[1]
    low = b_img.shape[1]
    assert rows == LANES and low == LANES
    img_bits, txt_bits = split_bits(n)
    img_span, txt_span = span(img_bits), span(txt_bits)
    ni, nt = len(img_span), len(txt_span)
    (img_emb,), img_inv = stream_embed([img_feats], w_img, False)
    far = gather(txt_feats, txt_bits[:-1], n)
    near = swap(txt_feats, txt_bits[-1], n)
    (txt_emb,), txt_inv, w_txt_v = stream_embed([txt_feats], w_txt, True)
    far = [txt_emb] + [embed([x], w_txt_v)[0] for x in far[1:]]
    onward = [swap(x, txt_bits[-1], n) for x in far[1:]]
    texts = far + embed([near], w_txt_v) + onward
    img_keys, txt_keys = call(
        keys_kernel,
        [((rows, a_img.shape[1] * LANES), F32), ((rows, a_txt.shape[1] * LANES), F32)],
        [img_feats, txt_feats, a_img.T, a_txt.T, img_inv, txt_inv],
        after=far[1:2],
    )
    images = gather(img_emb, img_bits, n, lambda x: hold(x, [texts[0], img_keys]))
    raw, *halfway = call(
        functools.partial(scores_kernel, ni - 1, nt - 1),
        [(((ni - 1) * rows, (nt - 1) * rows), F32)]
        + [(((ni - 1) * rows, 1), F32)] * 2
        + [((nt - 1, rows), F32)] * 2,
        images[:-1] + texts[:-1],
        scratch=[pltpu.VMEM(((ni - 1) * rows, wide), BF16), pltpu.VMEM(((nt - 1) * rows, wide), BF16)],
        flops=2 * (ni - 1) * (nt - 1) * rows * rows * wide,
    )
    last_col, last_row, row_lse, col_lse = call(
        functools.partial(last_scores_kernel, ni, nt),
        [(((ni - 1) * rows, rows), F32), ((rows, nt * rows), F32), ((ni, rows), F32), ((nt, rows), F32)],
        images + texts + halfway,
        scratch=[pltpu.VMEM(((ni - 1) * rows, wide), BF16), pltpu.VMEM((nt * rows, wide), BF16)],
        flops=2 * (ni + nt) * rows * rows * wide,
    )
    row_parts = gather(row_lse, img_bits, n)
    col_parts, col_flips = gather_lse(col_lse, txt_bits, n)
    img_low, img_side_t, txt_low, txt_side_t, img_base, txt_base = call(
        functools.partial(factors_kernel, ni, nt),
        [
            ((ni * rows, low), F32),
            ((low, ni * rows), BF16),
            ((nt * rows, low), BF16),
            ((low, nt * rows), F32),
            ((rows, low), F32),
            ((rows, low), F32),
        ],
        images + texts + [b_img, b_txt],
        flops=4 * (ni + nt) * rows * wide * low,
    )
    half = ni // 2
    *img_kept, img_sent, weights_bf, inners = call(
        functools.partial(weights_kernel, ni, nt, tuple(range(ni)), col_flips),
        [((rows, low), F32)] * half
        + [((half * rows, low), BF16), ((ni * rows, nt * rows), BF16), ((nt, rows), F32)],
        row_parts + col_parts + [raw, last_col, last_row, img_low, txt_low],
        flops=2 * ni * nt * rows * rows * low,
    )
    *txt_kept, txt_sent = call(
        functools.partial(columns_kernel, nt),
        [((rows, low), F32)] * (nt // 2) + [((nt // 2 * rows, low), BF16)],
        [weights_bf, inners, img_side_t, txt_side_t],
        flops=2 * ni * nt * rows * rows * low,
    )
    img_parts, _ = halve(img_kept, img_sent, img_bits, n)
    txt_parts, _ = halve(txt_kept, txt_sent, txt_bits, n)
    return (
        sketch(img_parts, img_base, img_keys, False),
        sketch(txt_parts, txt_base, txt_keys, True),
    )


def solution(mesh):
    n = mesh.shape["dp"]
    rows = P(("ckpt", "dp"), None)
    part = P("ckpt", None)
    return jax.shard_map(
        lambda *args: body(n, *args),
        mesh=mesh,
        in_specs=(rows, rows, part, part, P(), P(), P(), P()),
        out_specs=(rows, rows),
        check_vma=False,
    )
```
